256 devices in a mesh: level: 8 (over x, core), panel: 32 (over y, z).
Axes of the slice: x: 4, y: 4, z: 8, core: 2. Of those that a mesh axis runs over, the one named last changes fastest.
Arguments:
- contrib: bfloat16 [8, 8192, 8192], P('level', None, 'panel'), may hold values from -6 to 6
- pattern: int32 [8, 64, 64], P('level'), may hold values 0 or 1
- pivot_inverse: bfloat16 [8, 2, 128, 128], replicated, may hold values from -0.005859375 to 0.005859375
Outputs:
- schur: bfloat16 [8192, 8192], P('level', 'panel')
The draws below stay inside these ranges and needn't reach their ends.
All inputs are finite; a program needn't handle non-finite values. No bound on the sum of `pattern` on one device may be relied on, other than what follows from the above.
Results may differ from the reference program's by a relative error of at most 0.012.
Values may be sent and summed in bfloat16 or wider, within the bound.
A program may use at most 128 MiB of HBM per device.

```python
import jax
import jax.numpy as jnp

FRONT = 8192
PANEL = 128
SEP = 2
BLOCKS = 64
LEVELS = 3
N_LEVEL = 8


def touch_ends(drawn, own_key, smallest, largest):
    extent = drawn.shape
    spot = [jax.random.randint(jax.random.fold_in(own_key, axis), (), 0, extent[axis]) for axis in range(len(extent))]
    drawn = drawn.at[tuple(spot)].set(smallest)
    longest = extent.index(max(extent))
    spot[longest] = (spot[longest] + 1) % extent[longest]
    return drawn.at[tuple(spot)].set(largest)


def level_of(key, dims, split, least, largest):
    factor_of, own = 1.0, jax.random.fold_in(key, 6)
    for position, shards_of in split:
        steps = jnp.exp(jax.random.uniform(jax.random.fold_in(own, position), (shards_of,), jnp.float32, least / len(split), largest / len(split)))
        factor_of = factor_of * jnp.repeat(steps, dims[position] // shards_of).reshape([-1 if axis == position else 1 for axis in range(len(dims))])
    return factor_of


def bell_draw(rng, dims, width, reach, shards=(), held_as=jnp.bfloat16):
    drawn = jax.random.normal(rng, dims, jnp.float32) * width
    if len(shards) > 0:
        drawn = level_of(rng, dims, shards, -0.22, 0.18) * drawn
    return jnp.clip(drawn, min=-reach, max=reach).astype(held_as)


def setup_inputs(seed: int = 0) -> dict:
    keys = jax.random.split(jax.random.key(seed), 4)
    return {
        "contrib": bell_draw(keys[0], (N_LEVEL, FRONT, FRONT), 1.0, 6.0, ((0, 8), (2, 32))),
        "pattern": touch_ends((jax.random.randint(keys[1], (N_LEVEL, BLOCKS, BLOCKS), 0, 2) < 1).astype(jnp.int32), jax.random.fold_in(keys[1], 1), 0, 1),
        "pivot_inverse": bell_draw(keys[2], (N_LEVEL, SEP, PANEL, PANEL), (PANEL * PANEL * 64) ** -0.5, 0.005859375),
    }


def apply_pivot(front_mat, pivot_col, inverse, pivot_idx, col_panel):
    pivot_rows = front_mat[pivot_idx * PANEL:(pivot_idx + 1) * PANEL, :].astype(jnp.bfloat16)
    weights = jnp.dot(inverse, pivot_rows, preferred_element_type=jnp.float32)
    weights = jnp.where((col_panel > pivot_idx)[None, :], weights, 0.0).astype(jnp.bfloat16)
    return front_mat - jnp.dot(pivot_col, weights, preferred_element_type=jnp.float32)


def eliminate(front_mat, factors, tree_level, panel_index):
    sep_first = tree_level * SEP
    sep_end = sep_first + SEP
    is_sep = (panel_index >= sep_first) & (panel_index < sep_end)
    front_mat = jnp.where(is_sep[None, :], front_mat.astype(jnp.bfloat16).astype(jnp.float32), front_mat)
    for panel_step in range(SEP):
        pivot_idx = sep_first + panel_step
        column = front_mat[:, pivot_idx * PANEL:(pivot_idx + 1) * PANEL]
        pivot_col = jnp.where((panel_index > pivot_idx)[:, None], column, 0.0).astype(jnp.bfloat16)
        front_mat = apply_pivot(front_mat, pivot_col, factors[panel_step], pivot_idx, panel_index)
    keep_side = panel_index >= sep_end
    return jnp.where(keep_side[:, None] & keep_side[None, :], front_mat, 0.0).astype(jnp.bfloat16)


def reference(contrib, pattern, pivot_inverse):
    panel_index = (jnp.arange(FRONT) // PANEL).astype(jnp.int32)
    masked = contrib.reshape(N_LEVEL, BLOCKS, PANEL, BLOCKS, PANEL) * pattern.astype(jnp.bfloat16)[:, :, None, :, None]
    masked = masked.reshape(N_LEVEL, FRONT, FRONT)
    current = [masked[member] for member in range(N_LEVEL)]
    for tree_level in range(LEVELS):
        upper = []
        for subcube in range(len(current) // 2):
            front_mat = current[2 * subcube].astype(jnp.float32) + current[2 * subcube + 1].astype(jnp.float32)
            leader = (2 * subcube + 1) * 2 ** tree_level - 1
            upper.append(eliminate(front_mat, pivot_inverse[leader], tree_level, panel_index))
        current = upper
    return current[0]
```

```python
import functools

import jax
import jax.numpy as jnp
from jax import lax
from jax.experimental import pallas as pl
from jax.experimental.pallas import tpu as pltpu
from jax.sharding import PartitionSpec as P

MESH = pl.DeviceIdType.MESH
PANEL = 128
W = 256
SEP_END = 3 * W
NX, NC = 4, 2
ROWS = 1024
KC, KL = 8, 16
FLOWS = (
    (0, "A", 1),
    (0, "B", 1),
    (0, "A", -1),
    (0, "B", -1),
    (1, "A", 1),
    (1, "A", -1),
    (2, "B", 1),
    (2, "B", -1),
)
X_ORDER = (0, 1, 3, 2)
BF, F32 = jnp.bfloat16, jnp.float32


def dot(a, b):
    return jnp.dot(a, b, preferred_element_type=F32)


def pivots(sep, rows, inverse):
    first = dot(inverse[0], rows[:PANEL]).astype(BF)
    second_rows = (rows[PANEL:].astype(F32) - dot(sep[PANEL:, :PANEL], first)).astype(BF)
    second = dot(inverse[1], second_rows).astype(BF)
    between = dot(inverse[0], sep[:PANEL, PANEL:]).astype(BF)
    return jnp.concatenate([(first.astype(F32) - dot(between, second)).astype(BF), second], 0)


def kernel(
    ny, nz,
    pattern, contrib, inv, out,
    sent, own, xin, fin, trx, l0, l1, l2, c0, c1, c2, q, vx, acc,
    core_send, core_recv, trx_send, trx_recv, xin_send, xin_recv,
    fc_send, fc_recv, fl_send, fl_recv, q_send, q_recv,
):
    level, panel = lax.axis_index("level"), lax.axis_index("panel")
    x, c = level // NC, level % NC
    y, z = panel // nz, panel % nz
    other = (x * NC + 1 - c, panel)
    to_x = [(lax.rem(x + d, NX) * NC + c, panel) for d in (1, 3, 2)]
    to_y = {1: (level, lax.rem(y + 1, ny) * nz + z), -1: (level, lax.rem(y + ny - 1, ny) * nz + z)}
    to_z = {1: (level, y * nz + lax.rem(z + 1, nz)), -1: (level, y * nz + lax.rem(z + nz - 1, nz))}

    barrier = pltpu.get_barrier_semaphore()
    partners = [other] + to_x + [to_y[1], to_y[-1], to_z[1], to_z[-1]]
    for partner in partners:
        pl.semaphore_signal(barrier, inc=1, device_id=partner, device_id_type=MESH)
    pl.semaphore_wait(barrier, len(partners))

    def remote(src, dst, send, recv, device):
        return pltpu.make_async_remote_copy(
            src_ref=src, dst_ref=dst, send_sem=send, recv_sem=recv, device_id=device, device_id_type=MESH
        )

    lane = lax.broadcasted_iota(jnp.int32, (1, W), 1)

    def mask_block(target, j, parity):
        def step(i, carry):
            row = (j * NC + parity) * (ROWS // PANEL) + i
            left = pattern[row, panel * 2].astype(F32)
            right = pattern[row, panel * 2 + 1].astype(F32)
            factor = jnp.where(lane < PANEL, left, right)
            block = contrib[pl.ds(pl.multiple_of(row * PANEL, PANEL), PANEL), :].astype(F32) * factor
            target[j, pl.ds(pl.multiple_of(i * PANEL, PANEL), PANEL), :] = block.astype(BF)
            return carry

        lax.fori_loop(0, ROWS // PANEL, step, 0)

    core_copies = [remote(sent.at[j], fin.at[j], core_send.at[j], core_recv.at[j], other) for j in range(NX)]
    for j in range(NX):
        mask_block(sent, j, 1 - c)
        core_copies[j].start()
    for j in range(NX):
        mask_block(own, j, c)

    def add_block(j):
        core_copies[j].wait_recv()
        own[j] = (own[j].astype(F32) + fin[j].astype(F32)).astype(BF)

    add_block(0)
    trx_copies = [
        remote(own.at[0, pl.ds(0, SEP_END)], trx.at[x], trx_send.at[i], trx_recv.at[x], to_x[i]) for i in range(3)
    ]

    @pl.when(c == 0)
    def _():
        for copy in trx_copies:
            copy.start()

    for j in range(1, NX):
        add_block(j)
    xin_copies = []
    for i, d in enumerate((1, 3, 2)):
        there = lax.rem(x + d, NX)
        copy = remote(own.at[there], xin.at[x], xin_send.at[i], xin_recv.at[x], to_x[i])
        copy.start()
        xin_copies.append(copy)
    xin[x] = own[x]

    def wait_xin(there):
        remote(own.at[0], xin.at[there], xin_send.at[0], xin_recv.at[there], to_x[0]).wait_recv()

    @pl.when(c == 0)
    def _():
        trx[x] = own[0, :SEP_END]
        for d in (1, 3, 2):
            there = lax.rem(x + d, NX)
            remote(
                own.at[0, pl.ds(0, SEP_END)], trx.at[there], trx_send.at[0], trx_recv.at[there], to_x[0]
            ).wait_recv()

        @pl.when(panel == 0)
        def _():
            for i in range(NX):
                c0[i * SEP_END:(i + 1) * SEP_END] = trx[i]

        @pl.when(panel == 1)
        def _():
            for i in range(NX):
                c1[i * W:(i + 1) * W] = trx[i, :W]
            for g in range(2):
                total = trx[2 * g, W:].astype(F32) + trx[2 * g + 1, W:].astype(F32)
                c1[NX * W + g * 2 * W:NX * W + (g + 1) * 2 * W] = total.astype(BF)

        @pl.when(panel == 2)
        def _():
            for i in range(NX):
                c2[i * W:(i + 1) * W] = trx[i, :W]
            for g in range(2):
                total = trx[2 * g, W:2 * W].astype(F32) + trx[2 * g + 1, W:2 * W].astype(F32)
                c2[(NX + g) * W:(NX + g + 1) * W] = total.astype(BF)
            total = sum(trx[i, 2 * W:].astype(F32) for i in range(NX))
            c2[6 * W:] = total.astype(BF)

    def place(slab, kind, sign):
        if sign == 1:
            dy, dz = y, lax.rem(z - slab + nz, nz)
        else:
            dy, dz = lax.rem(ny - y, ny), lax.rem(slab - z + nz, nz)
        if kind == "A":
            depth = jnp.where(dy == 0, dz, jnp.where(dz >= 1, dz + dy, nz + dy))
            go_z = ((dy == 0) & (dz < nz - 1)) | ((dy >= 1) & (dz == nz - 1))
            go_y = (dz >= 1) & (dy < ny - 1)
        else:
            depth = jnp.where(dz == 0, dy, jnp.where(dy >= 1, dy + dz, ny + dz))
            go_y = ((dz == 0) & (dy < ny - 1)) | ((dz >= 1) & (dy == ny - 1))
            go_z = (dy >= 1) & (dz < nz - 1)
        return depth, go_y, go_z

    places = [place(*flow) for flow in FLOWS]
    part = {0: 0, 1: 0, 2: 0}
    tree = []
    for slab, _, _ in FLOWS:
        tree.append(part[slab])
        part[slab] += 1

    def top_item(f, k):
        slab, t = FLOWS[f][0], tree[f]
        if slab == 0:
            n = SEP_END // 4 // (KC // NX)
            row = (k // (KC // NX)) * SEP_END + t * (SEP_END // 4) + lax.rem(k, KC // NX) * n
            return c0.at[pl.ds(pl.multiple_of(row, 16), n)]
        ref, rows = (c1, 8 * W) if slab == 1 else (c2, 7 * W)
        n = rows // 2 // KC
        return ref.at[pl.ds(pl.multiple_of(t * (rows // 2) + k * n, 16), n)]

    def long_item(f, k):
        slab, t = FLOWS[f][0], tree[f]
        if slab == 0:
            per = KL // NX
            n = ROWS // 4 // per
            j = k // per
            there = lax.rem(x + jnp.where(j < 2, j, 5 - j), NX)
            row = there * ROWS + t * (ROWS // 4) + lax.rem(k, per) * n
            return l0.at[pl.ds(pl.multiple_of(row, 16), n)]
        if slab == 1:
            per = KL // 2
            n = ROWS // 2 // per
            row = (k // per) * ROWS + t * (ROWS // 2) + lax.rem(k, per) * n
            return l1.at[pl.ds(pl.multiple_of(row, 16), n)]
        n = ROWS // 2 // KL
        return l2.at[pl.ds(pl.multiple_of(t * (ROWS // 2) + k * n, 16), n)]

    def handle(f, k, item, send, recv):
        slab, _, sign = FLOWS[f]
        depth, go_y, go_z = places[f]
        ref = item(f, k)
        half = lax.rem(k, 2)

        @pl.when(depth > 0)
        def _():
            remote(ref, ref, send.at[f, 0, half], recv.at[f, k], to_z[sign]).wait_recv()

        for i, (go, device) in enumerate(((go_z, to_z[sign]), (go_y, to_y[sign]))):
            @pl.when(go)
            def _():
                copy = remote(ref, ref, send.at[f, i, half], recv.at[f, k], device)

                @pl.when(k >= 2)
                def _():
                    copy.wait_send()

                copy.start()

    def step(tau, carry):
        k_long = tau - KC

        @pl.when((panel == 0) & (k_long >= 0) & (k_long < KL) & (lax.rem(k_long + KL, KL // NX) == 0))
        def _():
            j = k_long // (KL // NX)
            there = lax.rem(x + jnp.where(j < 2, j, 5 - j), NX)

            @pl.when(j > 0)
            def _():
                wait_xin(there)

            l0[pl.ds(pl.multiple_of(there * ROWS, ROWS), ROWS), :] = xin[there]

        @pl.when(((panel == 1) | (panel == 2)) & (k_long == 0))
        def _():
            for d in (1, 3, 2):
                wait_xin(lax.rem(x + d, NX))

            @pl.when(panel == 1)
            def _():
                for g in range(2):
                    total = xin[2 * g].astype(F32) + xin[2 * g + 1].astype(F32)
                    l1[g * ROWS:(g + 1) * ROWS] = total.astype(BF)

            @pl.when(panel == 2)
            def _():
                l2[...] = sum(xin[i].astype(F32) for i in range(NX)).astype(BF)

        for f in range(len(FLOWS)):
            k = tau - places[f][0]

            @pl.when((c == 0) & (k >= 0) & (k < KC))
            def _():
                handle(f, k, top_item, fc_send, fc_recv)

            @pl.when((k >= KC) & (k < KC + KL))
            def _():
                handle(f, k - KC, long_item, fl_send, fl_recv)

        return carry

    lax.fori_loop(jnp.where(c == 0, 0, KC), KC + KL + ny + nz - 1, step, 0)

    for copy in core_copies + xin_copies:
        copy.wait_send()

    @pl.when(c == 0)
    def _():
        for copy in trx_copies:
            copy.wait_send()

    def drain(item, send, recv, count):
        for f, (slab, kind, sign) in enumerate(FLOWS):
            _, go_y, go_z = places[f]
            for i, (go, device) in enumerate(((go_z, to_z[sign]), (go_y, to_y[sign]))):
                @pl.when(go)
                def _():
                    for k in (count - 2, count - 1):
                        ref = item(f, k)
                        remote(ref, ref, send.at[f, i, k % 2], recv.at[f, k], device).wait_send()

    @pl.when(c == 0)
    def _():
        drain(top_item, fc_send, fc_recv, KC)

    drain(long_item, fl_send, fl_recv, KL)

    @pl.when(panel > 2)
    def _():
        for d in (1, 3, 2):
            wait_xin(lax.rem(x + d, NX))

    q_copy = remote(q, q, q_send, q_recv, other)

    @pl.when(c == 0)
    def _():
        for g in range(2):
            acc[g, :, :W] = c1[(4 + 2 * g) * W:(6 + 2 * g) * W].astype(F32)
            acc[g, :W, W:2 * W] = c2[(4 + g) * W:(5 + g) * W].astype(F32)
            acc[g, :W, 2 * W:] = trx[2 * g, W:2 * W].astype(F32) + trx[2 * g + 1, W:2 * W].astype(F32)
            acc[g, W:, W:] = jnp.zeros((W, 2 * W), F32)
            for i in (2 * g, 2 * g + 1):
                rows = jnp.concatenate(
                    [c1[i * W:(i + 1) * W], c2[i * W:(i + 1) * W], trx[i, :W]], axis=1
                )
                vx[i] = pivots(c0[i * SEP_END:i * SEP_END + W], rows, [inv[2 * i, 0], inv[2 * i, 1]])
                acc[g] -= dot(c0[i * SEP_END + W:(i + 1) * SEP_END], vx[i])
        last = [c2[6 * W:].astype(F32), sum(trx[i, 2 * W:].astype(F32) for i in range(NX))]
        last = jnp.concatenate(last, axis=1)
        vg = []
        for g in range(2):
            columns = acc[g, :, :W].astype(BF)
            vg.append(pivots(columns[:W], acc[g, :W, W:].astype(BF), [inv[4 * g + 1, 0], inv[4 * g + 1, 1]]))
            last = last + acc[g, W:, W:] - dot(columns[W:], vg[g])
        last = last.astype(BF)
        vh = pivots(last[:, :W], last[:, W:], [inv[3, 0], inv[3, 1]])
        q[6 * W:] = vh
        for g in range(2):
            qb = (vg[g][:, W:].astype(F32) - dot(vg[g][:, :W], vh)).astype(BF)
            q[(4 + g) * W:(5 + g) * W] = qb
            for i in (2 * g, 2 * g + 1):
                qa = vx[i, :, 2 * W:].astype(F32) - dot(vx[i, :, W:2 * W], vh) - dot(vx[i, :, :W], qb)
                q[i * W:(i + 1) * W] = qa.astype(BF)
        q_copy.start()
        q_copy.wait_send()

    @pl.when(c == 1)
    def _():
        q_copy.wait_recv()

    def finish(b, carry):
        n = 256
        here = pl.ds(pl.multiple_of(b * n, n), n)
        total = sum(xin[i, here].astype(F32) for i in range(NX))
        for i in range(7):
            if i < 4:
                block = l0[pl.ds(pl.multiple_of(i * ROWS + b * n, n), n), :]
            elif i < 6:
                block = l1[pl.ds(pl.multiple_of((i - 4) * ROWS + b * n, n), n), :]
            else:
                block = l2[here]
            total = total - dot(block, q[i * W:(i + 1) * W])
        kept = (panel > 2) & ((level > 0) | (b * n >= SEP_END))
        out[here, :] = jnp.where(kept, total, 0.0).astype(BF)
        return carry

    lax.fori_loop(0, ROWS // 256, finish, 0)


def solution(mesh):
    ny, nz = (4, 8) if mesh.shape["panel"] == 32 else (2, mesh.shape["panel"] // 2)

    def body(contrib, pattern, pivot_inverse):
        vmem = pl.BlockSpec(memory_space=pltpu.VMEM)
        dma = pltpu.SemaphoreType.DMA
        nf = len(FLOWS)
        return pl.pallas_call(
            functools.partial(kernel, ny, nz),
            out_shape=jax.ShapeDtypeStruct((ROWS, W), BF),
            in_specs=[pl.BlockSpec(memory_space=pltpu.SMEM), vmem, vmem],
            out_specs=vmem,
            scratch_shapes=[
                pltpu.VMEM((NX, ROWS, W), BF),
                pltpu.VMEM((NX, ROWS, W), BF),
                pltpu.VMEM((NX, ROWS, W), BF),
                pltpu.VMEM((NX, ROWS, W), BF),
                pltpu.VMEM((NX, SEP_END, W), BF),
                pltpu.VMEM((4 * ROWS, W), BF),
                pltpu.VMEM((2 * ROWS, W), BF),
                pltpu.VMEM((ROWS, W), BF),
                pltpu.VMEM((NX * SEP_END, W), BF),
                pltpu.VMEM((8 * W, W), BF),
                pltpu.VMEM((7 * W, W), BF),
                pltpu.VMEM((7 * W, W), BF),
                pltpu.VMEM((NX, W, 3 * W), BF),
                pltpu.VMEM((2, 2 * W, 3 * W), F32),
                dma((NX,)), dma((NX,)), dma((3,)), dma((NX,)), dma((3,)), dma((NX,)),
                dma((nf, 2, 2)), dma((nf, KC)), dma((nf, 2, 2)), dma((nf, KL)),
                dma, dma,
            ],
            compiler_params=pltpu.CompilerParams(
                collective_id=0, has_side_effects=True, vmem_limit_bytes=56 * 1024 * 1024
            ),
        )(pattern[0], contrib[0], pivot_inverse)

    in_specs = (P("level", None, "panel"), P("level", None, None), P())
    return jax.shard_map(body, mesh=mesh, in_specs=in_specs, out_specs=P("level", "panel"), check_vma=False)
```

```python
import functools

import jax
import jax.numpy as jnp
import numpy as np
from jax import lax
from jax.experimental import pallas as pl
from jax.experimental.pallas import tpu as pltpu
from jax.sharding import PartitionSpec as P

MESH = pl.DeviceIdType.MESH
PANEL = 128
W = 256
SEP_END = 3 * W
NX, NC, NY, NZ = 4, 2, 4, 8
ROWS = 1024
BF, F32 = jnp.bfloat16, jnp.float32
TREES = (
    ((0xFE000082, 0x657D0001, 0x07440000, 0xE1240000), (0x55AA55AA, 0xC6113992, 0x38FEFE7C)),
    ((0x0080100C, 0x0A80000E, 0x3810387F, 0x028B0600), (0x55AA55AA, 0xE776E4CC, 0xF8FDFBF0)),
    ((0x007DCF01, 0x0000FE00, 0x40080700, 0x0440E100), (0x55AA55AA, 0xBB93C692, 0xFE7C387C)),
    ((0x00022070, 0x900200F0, 0x80A3C000, 0x181018FD), (0x55AA55AA, 0xCFDC4E66, 0x3E7FBF1E)),
)
DEPTH = 7
FLOWS = tuple((slab, tree) for slab in range(3) for tree in range(4))
KO, KC = 4, 8
KL = 4 * KO
SLOTS = KL + KC
KS = (KL, 8, 8)
TOPS = (SEP_END // KC, 64, 64)
TOP_ITEMS = (KC, 8, 7)
SKEW = 3


def dot(a, b):
    return jnp.dot(a, b, preferred_element_type=F32)


def bit(mask, at):
    return lax.shift_right_logical(jnp.int32(np.uint32(mask).astype(np.int32)), at) & 1


def pivots(sep, rows, inverse):
    first = dot(inverse[0], rows[:PANEL]).astype(BF)
    second_rows = (rows[PANEL:].astype(F32) - dot(sep[PANEL:, :PANEL], first)).astype(BF)
    second = dot(inverse[1], second_rows).astype(BF)
    between = dot(inverse[0], sep[:PANEL, PANEL:]).astype(BF)
    return jnp.concatenate([(first.astype(F32) - dot(between, second)).astype(BF), second], 0)


def kernel(
    pattern, contrib, inv_in, out,
    raw, inv, sent, own, xin, fin, trx, l0, l1, l2, c0, c1, c2, q, vx, acc,
    load, core_send, core_recv, trx_send, trx_recv, xin_send, xin_recv,
    fc_send, fc_recv, fl_send, fl_recv, q_send, q_recv,
):
    level, panel = lax.axis_index("level"), lax.axis_index("panel")
    x, c = level // NC, level % NC
    y, z = panel // NZ, panel % NZ
    other = (x * NC + 1 - c, panel)
    apart = (1, 3, 2)
    to_x = [(lax.rem(x + d, NX) * NC + c, panel) for d in apart]
    to = [
        (level, lax.rem(y + 1, NY) * NZ + z),
        (level, lax.rem(y + NY - 1, NY) * NZ + z),
        (level, y * NZ + lax.rem(z + 1, NZ)),
        (level, y * NZ + lax.rem(z + NZ - 1, NZ)),
    ]

    def remote(src, dst, send, recv, device):
        return pltpu.make_async_remote_copy(
            src_ref=src, dst_ref=dst, send_sem=send, recv_sem=recv, device_id=device, device_id_type=MESH
        )

    def load_block(i):
        rows = pl.ds(pl.multiple_of((NC * (i % NX) + jnp.where(i < NX, 1 - c, c)) * ROWS, ROWS), ROWS)
        return pltpu.make_async_copy(contrib.at[rows], raw.at[rows], load.at[i])

    loads = [load_block(i) for i in range(2 * NX)]
    for copy in loads:
        copy.start()
    inv_load = pltpu.make_async_copy(inv_in, inv, load.at[2 * NX])
    inv_load.start()

    barrier = pltpu.get_barrier_semaphore()
    partners = [other] + to_x + to
    for partner in partners:
        pl.semaphore_signal(barrier, inc=1, device_id=partner, device_id_type=MESH)
    pl.semaphore_wait(barrier, len(partners))

    lane = lax.broadcasted_iota(jnp.int32, (1, W), 1)

    def mask_block(target, j, parity):
        def step(i, carry):
            row = (j * NC + parity) * (ROWS // PANEL) + i
            left = pattern[row, panel * 2].astype(F32)
            right = pattern[row, panel * 2 + 1].astype(F32)
            factor = jnp.where(lane < PANEL, left, right)
            block = raw[pl.ds(pl.multiple_of(row * PANEL, PANEL), PANEL), :].astype(F32) * factor
            target[j, pl.ds(pl.multiple_of(i * PANEL, PANEL), PANEL), :] = block.astype(BF)
            return carry

        lax.fori_loop(0, ROWS // PANEL, step, 0)

    core_copies = [remote(sent.at[j], fin.at[j], core_send.at[j], core_recv.at[j], other) for j in range(NX)]

    def add_block(j):
        core_copies[j].wait_recv()
        own[j] = (own[j].astype(F32) + fin[j].astype(F32)).astype(BF)

    top_rows = own.at[0, pl.ds(0, SEP_END)]
    trx_copies = [remote(top_rows, trx.at[x], trx_send.at[i], trx_recv.at[x], to_x[i]) for i in range(3)]
    xin_copies = [
        remote(own.at[lax.rem(x + d, NX)], xin.at[x], xin_send.at[i], xin_recv.at[x], to_x[i])
        for i, d in enumerate(apart)
    ]

    def core_phase():
        for j in range(NX):
            loads[j].wait()
            mask_block(sent, j, 1 - c)
            core_copies[j].start()
        for j in range(NX):
            loads[NX + j].wait()
            mask_block(own, j, c)
        add_block(0)

    def x_phase():
        @pl.when(c == 0)
        def _():
            for copy in trx_copies:
                copy.start()

        for j in range(1, NX):
            add_block(j)
        for copy in xin_copies:
            copy.start()
        xin[x] = own[x]

    def wait_xin(there):
        remote(own.at[0], xin.at[there], xin_send.at[0], xin_recv.at[there], to_x[0]).wait_recv()

    def wait_trx():
        trx[x] = own[0, :SEP_END]
        for d in apart:
            there = lax.rem(x + d, NX)
            remote(top_rows, trx.at[there], trx_send.at[0], trx_recv.at[there], to_x[0]).wait_recv()

    def top_blocks():
        wait_trx()

        @pl.when(panel == 0)
        def _():
            for i in range(NX):
                c0[i * SEP_END:(i + 1) * SEP_END] = trx[i]

        @pl.when(panel == 1)
        def _():
            for i in range(NX):
                c1[i * W:(i + 1) * W] = trx[i, :W]
            for g in range(2):
                total = trx[2 * g, W:].astype(F32) + trx[2 * g + 1, W:].astype(F32)
                c1[NX * W + g * 2 * W:NX * W + (g + 1) * 2 * W] = total.astype(BF)

        @pl.when(panel == 2)
        def _():
            for i in range(NX):
                c2[i * W:(i + 1) * W] = trx[i, :W]
            for g in range(2):
                total = trx[2 * g, W:2 * W].astype(F32) + trx[2 * g + 1, W:2 * W].astype(F32)
                c2[(NX + g) * W:(NX + g + 1) * W] = total.astype(BF)
            c2[6 * W:] = sum(trx[i, 2 * W:].astype(F32) for i in range(NX)).astype(BF)

    places = []
    for slab, tree in FLOWS:
        at = y * NZ + lax.rem(z - slab + NZ, NZ)
        go, deep = TREES[tree]
        depth = bit(deep[0], at) + 2 * bit(deep[1], at) + 4 * bit(deep[2], at)
        places.append((depth, [bit(mask, at) == 1 for mask in go]))

    def top_item(f, k):
        slab, tree = FLOWS[f]
        n = TOPS[slab]
        if slab == 0:
            per = KC // NX
            row = (k // per) * SEP_END + tree * (SEP_END // 4) + lax.rem(k, per) * n
        else:
            row = (tree * TOP_ITEMS[slab] + k) * n
        return (c0, c1, c2)[slab].at[pl.ds(pl.multiple_of(row, 16), n)]

    def long_item(f, k):
        slab, tree = FLOWS[f]
        fronts = (4, 2, 1)[slab]
        per = KS[slab] // fronts
        n = ROWS // 4 // per
        j = k // per
        if slab == 0:
            j = lax.rem(x + jnp.where(j < 2, j, 5 - j), NX)
        row = j * ROWS + tree * (ROWS // 4) + lax.rem(k, per) * n
        return (l0, l1, l2)[slab].at[pl.ds(pl.multiple_of(row, 16), n)]

    def handle(f, k, item, send, recv):
        depth, go = places[f]
        ref = item(f, k)
        half = lax.rem(k, 2)

        @pl.when(depth > 0)
        def _():
            remote(ref, ref, send.at[f, 0, half], recv.at[f, k], to[0]).wait_recv()

        for i in range(4):
            @pl.when(go[i])
            def _():
                copy = remote(ref, ref, send.at[f, i, half], recv.at[f, k], to[i])

                @pl.when(k >= 2)
                def _():
                    copy.wait_send()

                copy.start()

    def prepare(slot):
        @pl.when((c == 0) & (panel < 3) & (slot == KO))
        def _():
            top_blocks()

        @pl.when((panel == 0) & (slot == 0))
        def _():
            l0[pl.ds(pl.multiple_of(x * ROWS, ROWS), ROWS), :] = own[x]

        @pl.when((panel == 0) & (slot >= KO + KC) & (slot < SLOTS) & (lax.rem(slot - KC, KO) == 0))
        def _():
            j = (slot - KC) // KO
            there = lax.rem(x + jnp.where(j < 2, j, 5 - j), NX)
            wait_xin(there)
            l0[pl.ds(pl.multiple_of(there * ROWS, ROWS), ROWS), :] = xin[there]

        @pl.when((panel == 1) & (slot == SLOTS - KS[1]))
        def _():
            for d in apart:
                wait_xin(lax.rem(x + d, NX))
            for g in range(2):
                total = xin[2 * g].astype(F32) + xin[2 * g + 1].astype(F32)
                l1[g * ROWS:(g + 1) * ROWS] = total.astype(BF)

        @pl.when((panel == 2) & (slot == SLOTS - KS[2]))
        def _():
            for d in apart:
                wait_xin(lax.rem(x + d, NX))
            l2[...] = sum(xin[i].astype(F32) for i in range(NX)).astype(BF)

    def step(tau, carry):
        prepare(tau)
        for f, (slab, _) in enumerate(FLOWS):
            slot = tau - SKEW * places[f][0]

            @pl.when((c == 0) & (slot >= KO) & (slot < KO + TOP_ITEMS[slab]))
            def _():
                handle(f, slot - KO, top_item, fc_send, fc_recv)

            if slab == 0:
                is_long = ((slot >= 0) & (slot < KO)) | ((slot >= KO + KC) & (slot < SLOTS))
                k = jnp.where(slot < KO, slot, slot - KC)
            else:
                is_long = (slot >= SLOTS - KS[slab]) & (slot < SLOTS)
                k = slot - (SLOTS - KS[slab])

            @pl.when(is_long)
            def _():
                handle(f, k, long_item, fl_send, fl_recv)

        return carry

    def flows():
        lax.fori_loop(0, SLOTS + SKEW * DEPTH, step, 0)

        @pl.when((c == 0) & (panel > 2))
        def _():
            wait_trx()

        @pl.when(panel > 2)
        def _():
            for d in apart:
                wait_xin(lax.rem(x + d, NX))

    def drain(item, send, recv, counts):
        for f, (slab, _) in enumerate(FLOWS):
            go = places[f][1]
            for i in range(4):
                @pl.when(go[i])
                def _():
                    for k in (counts[slab] - 2, counts[slab] - 1):
                        ref = item(f, k)
                        remote(ref, ref, send.at[f, i, k % 2], recv.at[f, k], to[i]).wait_send()

    def drain_flows():
        @pl.when(c == 0)
        def _():
            drain(top_item, fc_send, fc_recv, TOP_ITEMS)

        drain(long_item, fl_send, fl_recv, KS)

    def drain_copies():
        for copy in core_copies + xin_copies:
            copy.wait_send()

        @pl.when(c == 0)
        def _():
            for copy in trx_copies:
                copy.wait_send()

    q_copy = remote(q, q, q_send, q_recv, other)

    def eliminate():
        for g in range(2):
            acc[g, :, :W] = c1[(4 + 2 * g) * W:(6 + 2 * g) * W].astype(F32)
            acc[g, :W, W:2 * W] = c2[(4 + g) * W:(5 + g) * W].astype(F32)
            acc[g, :W, 2 * W:] = trx[2 * g, W:2 * W].astype(F32) + trx[2 * g + 1, W:2 * W].astype(F32)
            acc[g, W:, W:] = jnp.zeros((W, 2 * W), F32)
            for i in (2 * g, 2 * g + 1):
                rows = jnp.concatenate(
                    [c1[i * W:(i + 1) * W], c2[i * W:(i + 1) * W], trx[i, :W]], axis=1
                )
                vx[i] = pivots(c0[i * SEP_END:i * SEP_END + W], rows, [inv[2 * i, 0], inv[2 * i, 1]])
                acc[g] -= dot(c0[i * SEP_END + W:(i + 1) * SEP_END], vx[i])
        last = [c2[6 * W:].astype(F32), sum(trx[i, 2 * W:].astype(F32) for i in range(NX))]
        last = jnp.concatenate(last, axis=1)
        vg = []
        for g in range(2):
            columns = acc[g, :, :W].astype(BF)
            vg.append(pivots(columns[:W], acc[g, :W, W:].astype(BF), [inv[4 * g + 1, 0], inv[4 * g + 1, 1]]))
            last = last + acc[g, W:, W:] - dot(columns[W:], vg[g])
        last = last.astype(BF)
        vh = pivots(last[:, :W], last[:, W:], [inv[3, 0], inv[3, 1]])
        q[6 * W:] = vh
        for g in range(2):
            qb = (vg[g][:, W:].astype(F32) - dot(vg[g][:, :W], vh)).astype(BF)
            q[(4 + g) * W:(5 + g) * W] = qb
            for i in (2 * g, 2 * g + 1):
                qa = vx[i, :, 2 * W:].astype(F32) - dot(vx[i, :, W:2 * W], vh) - dot(vx[i, :, :W], qb)
                q[i * W:(i + 1) * W] = qa.astype(BF)

    def factor_phase():
        inv_load.wait()

        @pl.when(c == 0)
        def _():
            eliminate()
            q_copy.start()
            q_copy.wait_send()

        @pl.when(c == 1)
        def _():
            q_copy.wait_recv()

    def finish(b, carry):
        n = 256
        here = pl.ds(pl.multiple_of(b * n, n), n)
        total = sum(xin[i, here].astype(F32) for i in range(NX))
        for i in range(7):
            if i < 4:
                block = l0[pl.ds(pl.multiple_of(i * ROWS + b * n, n), n), :]
            elif i < 6:
                block = l1[pl.ds(pl.multiple_of((i - 4) * ROWS + b * n, n), n), :]
            else:
                block = l2[here]
            total = total - dot(block, q[i * W:(i + 1) * W])
        kept = (panel > 2) & ((level > 0) | (b * n >= SEP_END))
        out[here, :] = jnp.where(kept, total, 0.0).astype(BF)
        return carry

    core_phase()
    x_phase()
    flows()
    drain_flows()
    drain_copies()
    factor_phase()
    lax.fori_loop(0, ROWS // 256, finish, 0)


def solution(mesh):
    def body(contrib, pattern, pivot_inverse):
        vmem = pl.BlockSpec(memory_space=pltpu.VMEM)
        anywhere = pl.BlockSpec(memory_space=pl.ANY)
        dma = pltpu.SemaphoreType.DMA
        nf = len(FLOWS)
        return pl.pallas_call(
            kernel,
            out_shape=jax.ShapeDtypeStruct((ROWS, W), BF),
            in_specs=[pl.BlockSpec(memory_space=pltpu.SMEM), anywhere, anywhere],
            out_specs=vmem,
            scratch_shapes=[
                pltpu.VMEM((2 * NX * ROWS, W), BF),
                pltpu.VMEM((8, 2, PANEL, PANEL), BF),
                pltpu.VMEM((NX, ROWS, W), BF),
                pltpu.VMEM((NX, ROWS, W), BF),
                pltpu.VMEM((NX, ROWS, W), BF),
                pltpu.VMEM((NX, ROWS, W), BF),
                pltpu.VMEM((NX, SEP_END, W), BF),
                pltpu.VMEM((4 * ROWS, W), BF),
                pltpu.VMEM((2 * ROWS, W), BF),
                pltpu.VMEM((ROWS, W), BF),
                pltpu.VMEM((NX * SEP_END, W), BF),
                pltpu.VMEM((8 * W, W), BF),
                pltpu.VMEM((7 * W, W), BF),
                pltpu.VMEM((7 * W, W), BF),
                pltpu.VMEM((NX, W, 3 * W), BF),
                pltpu.VMEM((2, 2 * W, 3 * W), F32),
                dma((2 * NX + 1,)), dma((NX,)), dma((NX,)), dma((3,)), dma((NX,)), dma((3,)), dma((NX,)),
                dma((nf, 4, 2)), dma((nf, KC)), dma((nf, 4, 2)), dma((nf, KL)),
                dma, dma,
            ],
            compiler_params=pltpu.CompilerParams(
                collective_id=0, has_side_effects=True, vmem_limit_bytes=56 * 1024 * 1024
            ),
        )(pattern[0], contrib[0], pivot_inverse)

    in_specs = (P("level", None, "panel"), P("level", None, None), P())
    return jax.shard_map(body, mesh=mesh, in_specs=in_specs, out_specs=P("level", "panel"), check_vma=False)
```

```python
import functools

import jax
import jax.numpy as jnp
import numpy as np
from jax import lax
from jax.experimental import pallas as pl
from jax.experimental.pallas import tpu as pltpu
from jax.sharding import PartitionSpec as P

MESH = pl.DeviceIdType.MESH
PANEL = 128
W = 256
SEP_END = 3 * W
NX, NC, NY, NZ = 4, 2, 4, 8
ROWS = 1024
BF, F32 = jnp.bfloat16, jnp.float32
TREES = (
    ((0xFE000082, 0x657D0001, 0x07440000, 0xE1240000), (0x55AA55AA, 0xC6113992, 0x38FEFE7C)),
    ((0x0080100C, 0x0A80000E, 0x3810387F, 0x028B0600), (0x55AA55AA, 0xE776E4CC, 0xF8FDFBF0)),
    ((0x007DCF01, 0x0000FE00, 0x40080700, 0x0440E100), (0x55AA55AA, 0xBB93C692, 0xFE7C387C)),
    ((0x00022070, 0x900200F0, 0x80A3C000, 0x181018FD), (0x55AA55AA, 0xCFDC4E66, 0x3E7FBF1E)),
)
DEPTH = 7
FIRST = tuple([mask & 1 for mask in go].index(1) for go, _ in TREES)
FLOWS = tuple((slab, tree) for slab in range(3) for tree in range(4))
KC = 4
LONG = (
    ((4, 5, 6, 7, 8, 9, 10, 11), (8, 9, 10, 11), (8, 10)),
    ((0, 1, 6, 7, 8, 9, 10, 11), (8, 9, 10, 11), (8, 10)),
)
TOPS = (0, 1, 2, 3)
CROSS = (0, 1, 2, 3)
HOPS = (6, 6)
SLOTS = 22
LAST = max(max(max(slots) for slots in LONG[i]) + (DEPTH - 1) * HOPS[i] // 2 for i in range(NC)) + 1
ELIMINATE = TOPS[-1] + 1 + (DEPTH - 1) * HOPS[0] // 2


def dot(a, b):
    return jnp.dot(a, b, preferred_element_type=F32)


def bit_of(word, at):
    return lax.shift_right_logical(word, at) & 1


def bit(mask, at):
    return bit_of(jnp.int32(np.uint32(mask).astype(np.int32)), at)


def at_slot(slots, core, slot):
    inside = (slot >= 0) & (slot < SLOTS)
    slot = jnp.clip(slot, 0, SLOTS - 1)
    taken = bit_of(jnp.where(core == 0, *[jnp.int32(sum(1 << t for t in own)) for own in slots]), slot) == 1
    words = [
        jnp.where(core == 0, *[jnp.int32(sum(k << 3 * (t % 10) for k, t in enumerate(own) if t // 10 == w)) for own in slots])
        for w in range(3)
    ]
    word = jnp.where(slot < 10, words[0], jnp.where(slot < 20, words[1], words[2]))
    return inside & taken, lax.shift_right_logical(word, 3 * lax.rem(slot, 10)) & 7


def pivots(fronts):
    seps, rows, inverses = zip(*fronts)
    n = range(len(fronts))
    first = [dot(inverses[i][0], rows[i][:PANEL]).astype(BF) for i in n]
    between = [dot(inverses[i][0], seps[i][:PANEL, PANEL:]).astype(BF) for i in n]
    second = [(rows[i][PANEL:].astype(F32) - dot(seps[i][PANEL:, :PANEL], first[i])).astype(BF) for i in n]
    second = [dot(inverses[i][1], second[i]).astype(BF) for i in n]
    first = [(first[i].astype(F32) - dot(between[i], second[i])).astype(BF) for i in n]
    return [jnp.concatenate([first[i], second[i]], 0) for i in n]


def kernel(
    pattern_in, contrib, inv_in, out,
    pattern, raw, inv, sent, own, xin, fin, trx, first_l, first_c, cross_l, cross_c,
    l0, l1, l2, c0, c1, c2, q, vx, vg, acc,
    load, core_send, core_recv, trx_send, trx_recv, xin_send, xin_recv,
    root_send, first_recv, cross_send, cross_recv, flow_send, c_recv, l_recv0, l_recv1, l_recv2, q_send, q_recv,
):
    level, panel = lax.axis_index("level"), lax.axis_index("panel")
    x, c = level // NC, level % NC
    y, z = panel // NZ, panel % NZ
    other = (x * NC + 1 - c, panel)
    apart = (1, 3, 2)
    theres = [lax.rem(x + d, NX) for d in apart]
    to_x = [(there * NC + c, panel) for there in theres]
    to = [
        (level, lax.rem(y + 1, NY) * NZ + z),
        (level, lax.rem(y + NY - 1, NY) * NZ + z),
        (level, y * NZ + lax.rem(z + 1, NZ)),
        (level, y * NZ + lax.rem(z + NZ - 1, NZ)),
    ]
    barrier = pltpu.get_barrier_semaphore()
    partners = [other] + to_x + to
    for partner in partners:
        pl.semaphore_signal(barrier, inc=1, device_id=partner, device_id_type=MESH)

    def remote(src, dst, send, recv, device):
        return pltpu.make_async_remote_copy(
            src_ref=src, dst_ref=dst, send_sem=send, recv_sem=recv, device_id=device, device_id_type=MESH
        )

    def load_block(i):
        rows = pl.ds(pl.multiple_of((NC * (i % NX) + jnp.where(i < NX, 1 - c, c)) * ROWS, ROWS), ROWS)
        return pltpu.make_async_copy(contrib.at[rows], raw.at[rows], load.at[i])

    pattern_load = pltpu.make_async_copy(pattern_in, pattern, load.at[2 * NX + 1])
    pattern_load.start()
    loads = [load_block(i) for i in range(2 * NX)]
    for copy in loads:
        copy.start()
    inv_load = pltpu.make_async_copy(inv_in, inv, load.at[2 * NX])
    inv_load.start()

    lane = lax.broadcasted_iota(jnp.int32, (1, W), 1)

    def mask_block(target, j, parity):
        def step(i, carry):
            row = (j * NC + parity) * (ROWS // PANEL) + i
            left = pattern[row, panel * 2].astype(F32)
            right = pattern[row, panel * 2 + 1].astype(F32)
            factor = jnp.where(lane < PANEL, left, right)
            block = raw[pl.ds(pl.multiple_of(row * PANEL, PANEL), PANEL), :].astype(F32) * factor
            target[j, i // 2, pl.ds(2 * lax.rem(i, 2), 2)] = block.astype(BF).reshape(2, 64, W)
            return carry

        lax.fori_loop(0, ROWS // PANEL, step, 0)

    core_copies = [remote(sent.at[j], fin.at[j], core_send.at[j], core_recv.at[j], other) for j in range(NX)]

    def add_block(j):
        core_copies[j].wait_recv()
        for h in range(4):
            own[j, h] = (own[j, h].astype(F32) + fin[j, h].astype(F32)).astype(BF)

    places = []
    for slab, tree in FLOWS:
        at = y * NZ + lax.rem(z - slab + NZ, NZ)
        go, deep = TREES[tree]
        depth = bit(deep[0], at) + 2 * bit(deep[1], at) + 4 * bit(deep[2], at)
        places.append((depth, [(bit(mask, at) == 1) & (depth > 0) for mask in go]))
    nexts = []
    for slab in range(3):
        firsts = [places[slab * 4 + tree][0] == 1 for tree in range(4)]
        nexts.append((sum(f.astype(jnp.int32) for f in firsts) > 0, sum(t * f.astype(jnp.int32) for t, f in enumerate(firsts))))
    root = jnp.minimum(panel, 2)

    top_rows = own.at[0, pl.ds(0, 3)]
    trx_copies = [remote(top_rows, trx.at[x], trx_send.at[i], trx_recv.at[x], to_x[i]) for i in range(3)]
    xin_copies = [
        remote(own.at[theres[i]], xin.at[x], xin_send.at[i], xin_recv.at[x], to_x[i]) for i in range(3)
    ]
    root_c = [
        remote(own.at[0, pl.ds(0, 3), t], first_c.at[root], root_send.at[t, NX], first_recv.at[root, NX], to[FIRST[t]])
        for t in range(4)
    ]
    root_l = [
        [
            remote(own.at[j, :, t], first_l.at[root, j], root_send.at[t, i], first_recv.at[root, j], to[FIRST[t]])
            for t in range(4)
        ]
        for i, j in enumerate([x] + theres)
    ]

    def core_phase():
        pattern_load.wait()
        for j in range(NX):
            loads[j].wait()
            mask_block(sent, j, 1 - c)
            if j == 0:
                pl.semaphore_wait(barrier, len(partners))
            core_copies[j].start()
        for j in range(NX):
            loads[NX + j].wait()
            mask_block(own, j, c)
        for j in range(NX):
            add_block(j)

        @pl.when(panel < 3)
        def _():
            @pl.when(c == 0)
            def _():
                for copy in root_c:
                    copy.start()

            for copies in root_l:
                for copy in copies:
                    copy.start()

    def cross_copy(slab, i):
        return remote(
            first_l.at[slab, theres[i]], cross_l.at[slab, x],
            cross_send.at[slab, 0, i], cross_recv.at[slab, 0, x], to_x[i],
        )

    def cross_copy_c(slab, i):
        return remote(
            first_c.at[slab], cross_c.at[slab, x], cross_send.at[slab, 1, i], cross_recv.at[slab, 1, x], to_x[i]
        )

    def wait_first(slab, j):
        remote(own.at[0, :, 0], first_l.at[slab, j], root_send.at[0, 0], first_recv.at[slab, j], to[0]).wait_recv()

    def wait_cross(slab, there):
        remote(
            first_l.at[slab, 0], cross_l.at[slab, there],
            cross_send.at[slab, 0, 0], cross_recv.at[slab, 0, there], to_x[0],
        ).wait_recv()

    def cross_step(slot):
        for slab in range(3):
            @pl.when(nexts[slab][0] & (c == 0) & (slot == CROSS[0]))
            def _():
                remote(
                    own.at[0, pl.ds(0, 3), 0], first_c.at[slab], root_send.at[0, 0], first_recv.at[slab, NX], to[0]
                ).wait_recv()
                for i in range(3):
                    cross_copy_c(slab, i).start()

            for i in range(3):
                @pl.when(nexts[slab][0] & (slot == CROSS[1 + i]))
                def _():
                    wait_first(slab, theres[i])
                    cross_copy(slab, i).start()

        @pl.when((panel > 2) & (slot == max(CROSS) + 1))
        def _():
            @pl.when(c == 0)
            def _():
                for copy in trx_copies:
                    copy.start()

            for copy in xin_copies:
                copy.start()

    def wait_sums():
        @pl.when(panel > 2)
        def _():
            xin[x] = own[x]
            for there in theres:
                remote(own.at[0], xin.at[there], xin_send.at[0], xin_recv.at[there], to_x[0]).wait_recv()

    def plus(*blocks):
        return sum(block.astype(F32) for block in blocks).astype(BF)

    def top_blocks(slab):
        tree = nexts[slab][1]
        cross_c[slab, x] = first_c[slab]
        for there in theres:
            remote(
                first_c.at[slab], cross_c.at[slab, there],
                cross_send.at[slab, 1, 0], cross_recv.at[slab, 1, there], to_x[0],
            ).wait_recv()
        if slab == 0:
            for i in range(NX):
                c0[i, :, tree] = cross_c[0, i]
            return
        ref = (c0, c1, c2)[slab]
        for i in range(NX):
            ref[i, tree] = cross_c[slab, i, 0]
        for g in range(2):
            if slab == 1:
                for h in range(2):
                    c1[4 + 2 * g + h, tree] = plus(cross_c[1, 2 * g, 1 + h], cross_c[1, 2 * g + 1, 1 + h])
            else:
                c2[4 + g, tree] = plus(cross_c[2, 2 * g, 1], cross_c[2, 2 * g + 1, 1])
        if slab == 2:
            c2[6, tree] = plus(*[cross_c[2, i, 2] for i in range(NX)])
            c2[7, tree] = jnp.zeros((64, W), BF)

    def long_sums(slab):
        tree = nexts[slab][1]
        wait_first(slab, x)
        cross_l[slab, x] = first_l[slab, x]
        for there in theres:
            wait_cross(slab, there)
        if slab == 1:
            for g in range(2):
                l1[g, :, tree] = plus(cross_l[1, 2 * g], cross_l[1, 2 * g + 1])
        else:
            l2[:, tree] = plus(*[cross_l[2, i] for i in range(NX)])

    def which(j):
        return lax.rem(x + jnp.where(j == 0, 0, jnp.where(j == 1, 3, j - 1)), NX)

    def prepare(slot):
        cross_step(slot)
        for slab in range(3):
            @pl.when((c == 0) & nexts[slab][0] & (slot == TOPS[0]))
            def _():
                top_blocks(slab)

        for j in range(NX):
            @pl.when(nexts[0][0] & (slot == jnp.where(c == 0, *[LONG[core][0][2 * j] for core in range(NC)])))
            def _():
                there = which(j)
                if j == 0:
                    wait_first(0, x)
                    l0[x, :, nexts[0][1]] = first_l[0, x]
                else:
                    wait_cross(0, there)
                    l0[there, :, nexts[0][1]] = cross_l[0, there]

        for slab in (1, 2):
            @pl.when(nexts[slab][0] & (slot == jnp.where(c == 0, *[LONG[core][slab][0] for core in range(NC)])))
            def _():
                long_sums(slab)

    def top_item(f, k):
        slab, tree = FLOWS[f]
        if slab == 0:
            return c0.at[k, :, tree]
        return (c0, c1, c2)[slab].at[pl.ds(2 * k, 2), tree]

    def long_item(f, k):
        slab, tree = FLOWS[f]
        here = pl.ds(2 * lax.rem(k, 2), 2)
        if slab == 0:
            return l0.at[which(k // 2), here, tree]
        if slab == 1:
            return l1.at[k // 2, here, tree]
        return l2.at[here, tree]

    def handle(f, k, item, recv, row):
        depth, go = places[f]
        ref = item(f, k)

        @pl.when(depth > 1)
        def _():
            remote(ref, ref, flow_send.at[f, 0], recv.at[row, k], to[0]).wait_recv()

        for i in range(4):
            @pl.when(go[i])
            def _():
                remote(ref, ref, flow_send.at[f, i], recv.at[row, k], to[i]).start()

    pieces = []
    hop = jnp.where(c == 0, *HOPS)

    def step(tau, carry):
        prepare(tau)
        for f, (slab, tree) in enumerate(FLOWS):
            depth = places[f][0]
            slot = tau - (depth - 1) * hop // 2
            is_top, k_top = at_slot((TOPS, TOPS), c, slot)
            is_long, k_long = at_slot((LONG[0][slab], LONG[1][slab]), c, slot)

            @pl.when((c == 0) & (depth > 0) & is_top)
            def _():
                handle(f, k_top, top_item, c_recv, f)

            @pl.when((depth > 0) & is_long)
            def _():
                handle(f, k_long, long_item, (l_recv0, l_recv1, l_recv2)[slab], tree)

        for i, piece in enumerate(pieces):
            when = min(ELIMINATE + i * (LAST - ELIMINATE) // len(pieces), LAST - 1)
            pl.when((c == 0) & (panel > 2) & (tau == when))(piece)
        return carry

    def flows():
        lax.fori_loop(0, LAST, step, 0)

    def drain_flows():
        for f, (slab, _) in enumerate(FLOWS):
            long_rows = (4, 2, 1)[slab] * ROWS // 4
            top = (SEP_END, 2 * W, 2 * W)[slab]
            for core, rows in ((0, long_rows + top), (1, long_rows)):
                for i in range(4):
                    @pl.when(places[f][1][i] & (c == core))
                    def _():
                        sized = raw.at[pl.ds(0, rows)]
                        remote(sized, sized, flow_send.at[f, i], c_recv.at[f, 0], to[i]).wait_send()

    q_copy = remote(q, q, q_send, q_recv, other)

    def drain_copies():
        for copy in core_copies:
            copy.wait_send()

        @pl.when(panel < 3)
        def _():
            for copies in root_l:
                for copy in copies:
                    copy.wait_send()

            @pl.when(c == 0)
            def _():
                for copy in root_c:
                    copy.wait_send()

        for slab in range(3):
            @pl.when(nexts[slab][0])
            def _():
                for i in range(3):
                    cross_copy(slab, i).wait_send()

                @pl.when(c == 0)
                def _():
                    for i in range(3):
                        cross_copy_c(slab, i).wait_send()

        @pl.when(panel > 2)
        def _():
            for copy in xin_copies:
                copy.wait_send()

            @pl.when(c == 0)
            def _():
                q_copy.wait_send()
                for copy in trx_copies:
                    copy.wait_send()

    def flat(block):
        return block.reshape(-1, W)

    def wait_top():
        inv_load.wait()
        trx[x] = own[0, :3]
        for there in theres:
            remote(top_rows, trx.at[there], trx_send.at[0], trx_recv.at[there], to_x[0]).wait_recv()

    def front_weights(g):
        pair = (2 * g, 2 * g + 1)
        fronts = []
        for i in pair:
            rows = jnp.concatenate([flat(c1[i]), flat(c2[i]), flat(trx[i, 0])], axis=1)
            fronts.append((flat(c0[i, 0]), rows, [inv[2 * i, 0], inv[2 * i, 1]]))
        for i, weights in zip(pair, pivots(fronts)):
            vx[i] = weights

    def front_update(i):
        g = i // 2
        if i % 2 == 0:
            acc[g, :, :W] = flat(c1[4 + 2 * g:6 + 2 * g]).astype(F32)
            acc[g, :W, W:2 * W] = flat(c2[4 + g]).astype(F32)
            acc[g, :W, 2 * W:] = flat(trx[2 * g, 1]).astype(F32) + flat(trx[2 * g + 1, 1]).astype(F32)
            acc[g, W:, W:] = jnp.zeros((W, 2 * W), F32)
        acc[g] -= dot(flat(c0[i, 1:]), vx[i])

    def pair_weights():
        columns = [acc[g, :, :W].astype(BF) for g in range(2)]
        fronts = [
            (columns[g][:W], acc[g, :W, W:].astype(BF), [inv[4 * g + 1, 0], inv[4 * g + 1, 1]]) for g in range(2)
        ]
        for g, weights in enumerate(pivots(fronts)):
            vg[g] = weights
            acc[g, W:, W:] -= dot(columns[g][W:], weights)

    def last_weights():
        last = [flat(c2[6]).astype(F32), sum(flat(trx[i, 2]).astype(F32) for i in range(NX))]
        last = (jnp.concatenate(last, axis=1) + acc[0, W:, W:] + acc[1, W:, W:]).astype(BF)
        q[6 * W:] = pivots([(last[:, :W], last[:, W:], [inv[3, 0], inv[3, 1]])])[0]

    def pair_factor():
        vh = q[6 * W:]
        for g in range(2):
            q[(4 + g) * W:(5 + g) * W] = (vg[g, :, W:].astype(F32) - dot(vg[g, :, :W], vh)).astype(BF)

    def front_factor(g):
        vh, qb = q[6 * W:], q[(4 + g) * W:(5 + g) * W]
        for i in (2 * g, 2 * g + 1):
            total = vx[i, :, 2 * W:].astype(F32) - dot(vx[i, :, W:2 * W], vh)
            q[i * W:(i + 1) * W] = (total - dot(vx[i, :, :W], qb)).astype(BF)

    pieces.append(wait_top)
    for g in range(2):
        pieces.append(functools.partial(front_weights, g))
        pieces += [functools.partial(front_update, 2 * g + i) for i in range(2)]
    pieces += [pair_weights, last_weights, pair_factor]
    pieces += [functools.partial(front_factor, g) for g in range(2)] + [q_copy.start]

    def finish(b, carry):
        n = 256
        total = sum(flat(xin[i, b]).astype(F32) for i in range(NX))
        for i in range(7):
            block = l0[i, b] if i < 4 else l1[i - 4, b] if i < 6 else l2[b]
            total = total - dot(flat(block), q[i * W:(i + 1) * W])
        kept = (level > 0) | (b * n >= SEP_END)
        out[pl.ds(pl.multiple_of(b * n, n), n), :] = jnp.where(kept, total, 0.0).astype(BF)
        return carry

    def result():
        @pl.when(panel < 3)
        def _():
            inv_load.wait()
            out[...] = jnp.zeros_like(out)

        @pl.when(panel > 2)
        def _():
            @pl.when(c == 1)
            def _():
                inv_load.wait()
                q_copy.wait_recv()

            lax.fori_loop(0, ROWS // 256, finish, 0)

    core_phase()
    flows()
    wait_sums()
    result()
    drain_flows()
    drain_copies()


def solution(mesh):
    def body(contrib, pattern, pivot_inverse):
        anywhere = pl.BlockSpec(memory_space=pl.ANY)
        dma = pltpu.SemaphoreType.DMA
        nf = len(FLOWS)

        def rows(*sizes):
            return pltpu.VMEM((*sizes, 64, W), BF)

        return pl.pallas_call(
            kernel,
            out_shape=jax.ShapeDtypeStruct((ROWS, W), BF),
            in_specs=[anywhere] * 3,
            out_specs=pl.BlockSpec(memory_space=pltpu.VMEM),
            scratch_shapes=[
                pltpu.SMEM((64, 64), jnp.int32),
                pltpu.VMEM((2 * NX * ROWS, W), BF),
                pltpu.VMEM((8, 2, PANEL, PANEL), BF),
                rows(NX, 4, 4), rows(NX, 4, 4), rows(NX, 4, 4), rows(NX, 4, 4), rows(NX, 3, 4),
                rows(3, NX, 4), rows(3, 3), rows(3, NX, 4), rows(3, NX, 3),
                rows(4, 4, 4), rows(2, 4, 4), rows(4, 4), rows(NX, 3, 4), rows(8, 4), rows(8, 4),
                pltpu.VMEM((7 * W, W), BF),
                pltpu.VMEM((NX, W, 3 * W), BF),
                pltpu.VMEM((2, W, 2 * W), BF),
                pltpu.VMEM((2, 2 * W, 3 * W), F32),
                dma((2 * NX + 2,)), dma((NX,)), dma((NX,)), dma((3,)), dma((NX,)), dma((3,)), dma((NX,)),
                dma((4, NX + 1)), dma((3, NX + 1)), dma((3, 2, 3)), dma((3, 2, NX)),
                dma((nf, 4)), dma((nf, KC)), dma((4, 8)), dma((4, 4)), dma((4, 2)),
                dma, dma,
            ],
            compiler_params=pltpu.CompilerParams(
                collective_id=0, has_side_effects=True, vmem_limit_bytes=56 * 1024 * 1024
            ),
        )(pattern[0], contrib[0], pivot_inverse)

    in_specs = (P("level", None, "panel"), P("level", None, None), P())
    return jax.shard_map(body, mesh=mesh, in_specs=in_specs, out_specs=P("level", "panel"), check_vma=False)
```

```python
import functools

import jax
import jax.numpy as jnp
import numpy as np
from jax import lax
from jax.experimental import pallas as pl
from jax.experimental.pallas import tpu as pltpu
from jax.sharding import PartitionSpec as P

MESH = pl.DeviceIdType.MESH
PANEL = 128
W = 256
SEP_END = 3 * W
NX, NC, NY, NZ = 4, 2, 4, 8
ROWS = 1024
BF, F32 = jnp.bfloat16, jnp.float32
TREES = (
    ((0xFE000082, 0x657D0001, 0x07440000, 0xE1240000), (0x55AA55AA, 0xC6113992, 0x38FEFE7C)),
    ((0x0080100C, 0x0A80000E, 0x3810387F, 0x028B0600), (0x55AA55AA, 0xE776E4CC, 0xF8FDFBF0)),
    ((0x007DCF01, 0x0000FE00, 0x40080700, 0x0440E100), (0x55AA55AA, 0xBB93C692, 0xFE7C387C)),
    ((0x00022070, 0x900200F0, 0x80A3C000, 0x181018FD), (0x55AA55AA, 0xCFDC4E66, 0x3E7FBF1E)),
)
DEPTH = 7
FIRST = tuple([mask & 1 for mask in go].index(1) for go, _ in TREES)
FLOWS = tuple((slab, tree) for slab in range(3) for tree in range(4))
KC = 4
LONG = (
    ((5, 6, 7, 8, 9, 10, 11, 12), (9, 10, 11, 12), (9, 11)),
    ((0, 1, 6, 7, 8, 9, 10, 11), (8, 9, 10, 11), (8, 10)),
)
TOPS = ((0, 1, 2, 3), (1, 2, 3, 4), (1, 2, 3, 4))
CROSS = (0, 1, 2, 3)
HOPS = (6, 4)
SLOTS = 22
LAST = max(max(max(slots) for slots in LONG[i]) + (DEPTH - 1) * HOPS[i] // 2 for i in range(NC)) + 1
ELIMINATE = max(max(slots) for slots in TOPS) + 1 + (DEPTH - 1) * HOPS[0] // 2
UNROLL = 1
SPREAD = 3


def dot(a, b):
    return jnp.dot(a, b, preferred_element_type=F32)


def bit_of(word, at):
    return lax.shift_right_logical(word, at) & 1


def bit(mask, at):
    return bit_of(jnp.int32(np.uint32(mask).astype(np.int32)), at)


def at_slot(slots, core, slot):
    taken = bit_of(jnp.where(core == 0, *[jnp.int32(sum(1 << t for t in own)) for own in slots]), slot) == 1
    words = [
        jnp.where(core == 0, *[jnp.int32(sum(k << 3 * (t % 10) for k, t in enumerate(own) if t // 10 == w)) for own in slots])
        for w in range(3)
    ]
    word = jnp.where(slot < 10, words[0], jnp.where(slot < 20, words[1], words[2]))
    return taken, lax.shift_right_logical(word, 3 * lax.rem(slot, 10)) & 7


def pivots(fronts):
    seps, rows, inverses = zip(*fronts)
    n = range(len(fronts))
    first = [dot(inverses[i][0], rows[i][:PANEL]).astype(BF) for i in n]
    between = [dot(inverses[i][0], seps[i][:PANEL, PANEL:]).astype(BF) for i in n]
    second = [(rows[i][PANEL:].astype(F32) - dot(seps[i][PANEL:, :PANEL], first[i])).astype(BF) for i in n]
    second = [dot(inverses[i][1], second[i]).astype(BF) for i in n]
    first = [(first[i].astype(F32) - dot(between[i], second[i])).astype(BF) for i in n]
    return [jnp.concatenate([first[i], second[i]], 0) for i in n]


def kernel(
    pattern_in, contrib, inv_in, out,
    pattern, raw, inv, sent, own, xin, fin, trx, first_l, first_c, cross_l, cross_c,
    l0, l1, l2, c0, c1, c2, q, vx, vg, acc,
    load, core_send, core_recv, trx_send, trx_recv, xin_send, xin_recv,
    root_send, first_recv, cross_send, cross_recv, flow_send, c_recv, l_recv0, l_recv1, l_recv2, q_send, q_recv,
):
    level, panel = lax.axis_index("level"), lax.axis_index("panel")
    x, c = level // NC, level % NC
    y, z = panel // NZ, panel % NZ
    other = (x * NC + 1 - c, panel)
    apart = (1, 3, 2)
    theres = [lax.rem(x + d, NX) for d in apart]
    to_x = [(there * NC + c, panel) for there in theres]
    to = [
        (level, lax.rem(y + 1, NY) * NZ + z),
        (level, lax.rem(y + NY - 1, NY) * NZ + z),
        (level, y * NZ + lax.rem(z + 1, NZ)),
        (level, y * NZ + lax.rem(z + NZ - 1, NZ)),
    ]
    barrier = pltpu.get_barrier_semaphore()
    partners = [other] + to_x + to
    for partner in partners:
        pl.semaphore_signal(barrier, inc=1, device_id=partner, device_id_type=MESH)

    def remote(src, dst, send, recv, device):
        return pltpu.make_async_remote_copy(
            src_ref=src, dst_ref=dst, send_sem=send, recv_sem=recv, device_id=device, device_id_type=MESH
        )

    near = [x] + theres
    top_at = jnp.where(x == 0, 0, jnp.where(x == 3, 1, jnp.where(x == 1, 2, 3)))
    order = [0] + [jnp.where(top_at >= n, near[n - 1], near[n]) for n in range(1, NX)]

    def load_block(i):
        rows = pl.ds(pl.multiple_of((NC * order[i % NX] + jnp.where(i < NX, 1 - c, c)) * ROWS, ROWS), ROWS)
        return pltpu.make_async_copy(contrib.at[rows], raw.at[rows], load.at[i])

    pattern_load = pltpu.make_async_copy(pattern_in, pattern, load.at[2 * NX + 1])
    pattern_load.start()
    loads = [load_block(i) for i in range(2 * NX)]
    for copy in loads:
        copy.start()
    inv_load = pltpu.make_async_copy(inv_in, inv, load.at[2 * NX])
    inv_load.start()

    lane = lax.broadcasted_iota(jnp.int32, (PANEL, W), 1)

    def mask_block(j, parity, store):
        def step(i, carry):
            row = (j * NC + parity) * (ROWS // PANEL) + i
            left = pattern[row, panel * 2].astype(F32)
            right = pattern[row, panel * 2 + 1].astype(F32)
            factor = jnp.where(lane < PANEL, left, right).astype(BF)
            block = raw[pl.ds(pl.multiple_of(row * PANEL, PANEL), PANEL), :] * factor
            store(i // 2, pl.ds(2 * lax.rem(i, 2), 2), block.reshape(2, 64, W))
            return carry

        lax.fori_loop(0, ROWS // PANEL, step, 0, unroll=UNROLL)

    core_copies = [remote(sent.at[j], fin.at[j], core_send.at[n], core_recv.at[n], other) for n, j in enumerate(order)]

    def send_block(n):
        def store(h, half, block):
            sent[order[n], h, half] = block

        loads[n].wait()
        mask_block(order[n], 1 - c, store)
        if n == 0:
            pl.semaphore_wait(barrier, len(partners))
        core_copies[n].start()

    def add_block(n):
        def store(h, half, block):
            own[order[n], h, half] = block + fin[order[n], h, half]

        loads[NX + n].wait()
        core_copies[n].wait_recv()
        mask_block(order[n], c, store)

    places = []
    for slab, tree in FLOWS:
        at = y * NZ + lax.rem(z - slab + NZ, NZ)
        go, deep = TREES[tree]
        depth = bit(deep[0], at) + 2 * bit(deep[1], at) + 4 * bit(deep[2], at)
        places.append((depth, [(bit(mask, at) == 1) & (depth > 0) for mask in go]))
    nexts = []
    for slab in range(3):
        firsts = [places[slab * 4 + tree][0] == 1 for tree in range(4)]
        nexts.append((sum(f.astype(jnp.int32) for f in firsts) > 0, sum(t * f.astype(jnp.int32) for t, f in enumerate(firsts))))
    root = jnp.minimum(panel, 2)

    top_rows = own.at[0, pl.ds(0, 3)]
    trx_copies = [remote(top_rows, trx.at[x], trx_send.at[i], trx_recv.at[x], to_x[i]) for i in range(3)]
    xin_copies = [
        remote(own.at[theres[i]], xin.at[x], xin_send.at[i], xin_recv.at[x], to_x[i]) for i in range(3)
    ]
    root_c = [
        remote(own.at[0, pl.ds(0, 3), t], first_c.at[root], root_send.at[t, NX], first_recv.at[root, NX], to[FIRST[t]])
        for t in range(4)
    ]
    root_l = [
        [
            remote(own.at[j, :, t], first_l.at[root, j], root_send.at[t, n], first_recv.at[root, j], to[FIRST[t]])
            for t in range(4)
        ]
        for n, j in enumerate(order)
    ]

    def core_phase():
        pattern_load.wait()
        for n in range(NX):
            send_block(n)
        for n in range(NX):
            add_block(n)

            @pl.when(panel < 3)
            def _():
                if n == 0:
                    @pl.when(c == 0)
                    def _():
                        for copy in root_c:
                            copy.start()

                for copy in root_l[n]:
                    copy.start()

    def cross_copy(slab, i):
        return remote(
            first_l.at[slab, theres[i]], cross_l.at[slab, x],
            cross_send.at[slab, 0, i], cross_recv.at[slab, 0, x], to_x[i],
        )

    def cross_copy_c(slab, i):
        return remote(
            first_c.at[slab], cross_c.at[slab, x], cross_send.at[slab, 1, i], cross_recv.at[slab, 1, x], to_x[i]
        )

    def wait_first(slab, j):
        remote(own.at[0, :, 0], first_l.at[slab, j], root_send.at[0, 0], first_recv.at[slab, j], to[0]).wait_recv()

    def wait_cross(slab, there):
        remote(
            first_l.at[slab, 0], cross_l.at[slab, there],
            cross_send.at[slab, 0, 0], cross_recv.at[slab, 0, there], to_x[0],
        ).wait_recv()

    def cross_step(slot):
        for slab in range(3):
            @pl.when(nexts[slab][0] & (c == 0) & (slot == CROSS[0]))
            def _():
                remote(
                    own.at[0, pl.ds(0, 3), 0], first_c.at[slab], root_send.at[0, 0], first_recv.at[slab, NX], to[0]
                ).wait_recv()
                for i in range(3):
                    cross_copy_c(slab, i).start()

            for i in range(3):
                @pl.when(nexts[slab][0] & (slot == CROSS[1 + i]))
                def _():
                    wait_first(slab, theres[i])
                    cross_copy(slab, i).start()

    def x_start():
        @pl.when(c == 0)
        def _():
            for copy in trx_copies:
                copy.start()

        for copy in xin_copies:
            copy.start()

    def wait_sums():
        @pl.when(panel > 2)
        def _():
            xin[x] = own[x]
            for there in theres:
                remote(own.at[0], xin.at[there], xin_send.at[0], xin_recv.at[there], to_x[0]).wait_recv()

    def plus(*blocks):
        return sum(block.astype(F32) for block in blocks).astype(BF)

    def wait_cross_c(slab, there):
        remote(
            first_c.at[slab], cross_c.at[slab, there],
            cross_send.at[slab, 1, 0], cross_recv.at[slab, 1, there], to_x[0],
        ).wait_recv()

    def top_blocks(slab):
        tree = nexts[slab][1]
        cross_c[slab, x] = first_c[slab]
        for there in theres:
            wait_cross_c(slab, there)
        ref = (c0, c1, c2)[slab]
        for i in range(NX):
            ref[i, tree] = cross_c[slab, i, 0]
        for g in range(2):
            if slab == 1:
                for h in range(2):
                    c1[4 + 2 * g + h, tree] = plus(cross_c[1, 2 * g, 1 + h], cross_c[1, 2 * g + 1, 1 + h])
            else:
                c2[4 + g, tree] = plus(cross_c[2, 2 * g, 1], cross_c[2, 2 * g + 1, 1])
        if slab == 2:
            c2[6, tree] = plus(*[cross_c[2, i, 2] for i in range(NX)])
            c2[7, tree] = jnp.zeros((64, W), BF)

    def long_sums(slab):
        tree = nexts[slab][1]
        wait_first(slab, x)
        cross_l[slab, x] = first_l[slab, x]
        for there in theres:
            wait_cross(slab, there)
        if slab == 1:
            for g in range(2):
                l1[g, :, tree] = plus(cross_l[1, 2 * g], cross_l[1, 2 * g + 1])
        else:
            l2[:, tree] = plus(*[cross_l[2, i] for i in range(NX)])

    def which(j):
        return lax.rem(x + jnp.where(j == 0, 0, jnp.where(j == 1, 3, j - 1)), NX)

    def prepare(slot):
        cross_step(slot)
        for j in range(NX):
            @pl.when((c == 0) & nexts[0][0] & (slot == TOPS[0][j]))
            def _():
                there = which(j)
                if j == 0:
                    c0[x, :, nexts[0][1]] = first_c[0]
                else:
                    wait_cross_c(0, there)
                    c0[there, :, nexts[0][1]] = cross_c[0, there]

        for slab in (1, 2):
            @pl.when((c == 0) & nexts[slab][0] & (slot == TOPS[slab][0]))
            def _():
                top_blocks(slab)

        for j in range(NX):
            @pl.when(nexts[0][0] & (slot == jnp.where(c == 0, *[LONG[core][0][2 * j] for core in range(NC)])))
            def _():
                there = which(j)
                if j == 0:
                    wait_first(0, x)
                    l0[x, :, nexts[0][1]] = first_l[0, x]
                else:
                    wait_cross(0, there)
                    l0[there, :, nexts[0][1]] = cross_l[0, there]

        for slab in (1, 2):
            @pl.when(nexts[slab][0] & (slot == jnp.where(c == 0, *[LONG[core][slab][0] for core in range(NC)])))
            def _():
                long_sums(slab)

    def top_item(f, k):
        slab, tree = FLOWS[f]
        if slab == 0:
            return c0.at[which(k), :, tree]
        return (c0, c1, c2)[slab].at[pl.ds(2 * k, 2), tree]

    def long_item(f, k):
        slab, tree = FLOWS[f]
        here = pl.ds(2 * lax.rem(k, 2), 2)
        if slab == 0:
            return l0.at[which(k // 2), here, tree]
        if slab == 1:
            return l1.at[k // 2, here, tree]
        return l2.at[here, tree]

    def handle(f, k, item, recv, row):
        depth, go = places[f]
        ref = item(f, k)

        @pl.when(depth > 1)
        def _():
            remote(ref, ref, flow_send.at[f, 0], recv.at[row, k], to[0]).wait_recv()

        for i in range(4):
            @pl.when(go[i])
            def _():
                remote(ref, ref, flow_send.at[f, i], recv.at[row, k], to[i]).start()

    pieces = []
    is_first = nexts[0][0] | nexts[1][0] | nexts[2][0]
    hop = jnp.where(c == 0, *HOPS)

    def step(tau, carry):
        pl.when(is_first & (tau < SLOTS))(functools.partial(prepare, tau))
        pl.when((panel > 2) & (tau == max(CROSS) + 1))(x_start)
        for f, (slab, tree) in enumerate(FLOWS):
            depth = places[f][0]
            slot = tau - (depth - 1) * hop // 2

            @pl.when((depth > 0) & (slot >= 0) & (slot < SLOTS))
            def _():
                is_top, k_top = at_slot((TOPS[slab],) * NC, c, slot)
                is_long, k_long = at_slot((LONG[0][slab], LONG[1][slab]), c, slot)

                @pl.when((c == 0) & is_top)
                def _():
                    handle(f, k_top, top_item, c_recv, f)

                @pl.when(is_long)
                def _():
                    handle(f, k_long, long_item, (l_recv0, l_recv1, l_recv2)[slab], tree)

        @pl.when((c == 0) & (panel > 2) & (tau >= ELIMINATE))
        def _():
            for i, piece in enumerate(pieces):
                when = min(ELIMINATE + i * SPREAD // len(pieces), LAST - 1)
                pl.when(tau == when)(piece)

        return carry

    def flows():
        lax.fori_loop(0, LAST, step, 0)

    def drain_flows():
        for f, (slab, _) in enumerate(FLOWS):
            long_rows = (4, 2, 1)[slab] * ROWS // 4
            top = (SEP_END, 2 * W, 2 * W)[slab]
            for core, rows in ((0, long_rows + top), (1, long_rows)):
                for i in range(4):
                    @pl.when(places[f][1][i] & (c == core))
                    def _():
                        sized = raw.at[pl.ds(0, rows)]
                        remote(sized, sized, flow_send.at[f, i], c_recv.at[f, 0], to[i]).wait_send()

    q_copy = remote(q, q, q_send, q_recv, other)

    def drain_copies():
        for copy in core_copies:
            copy.wait_send()

        @pl.when(panel < 3)
        def _():
            for copies in root_l:
                for copy in copies:
                    copy.wait_send()

            @pl.when(c == 0)
            def _():
                for copy in root_c:
                    copy.wait_send()

        for slab in range(3):
            @pl.when(nexts[slab][0])
            def _():
                for i in range(3):
                    cross_copy(slab, i).wait_send()

                @pl.when(c == 0)
                def _():
                    for i in range(3):
                        cross_copy_c(slab, i).wait_send()

        @pl.when(panel > 2)
        def _():
            for copy in xin_copies:
                copy.wait_send()

            @pl.when(c == 0)
            def _():
                q_copy.wait_send()
                for copy in trx_copies:
                    copy.wait_send()

    def flat(block):
        return block.reshape(-1, W)

    def wait_top():
        inv_load.wait()
        trx[x] = own[0, :3]
        for there in theres:
            remote(top_rows, trx.at[there], trx_send.at[0], trx_recv.at[there], to_x[0]).wait_recv()

    def front_weights(g):
        pair = (2 * g, 2 * g + 1)
        fronts = []
        for i in pair:
            rows = jnp.concatenate([flat(c1[i]), flat(c2[i]), flat(trx[i, 0])], axis=1)
            fronts.append((flat(c0[i, 0]), rows, [inv[2 * i, 0], inv[2 * i, 1]]))
        for i, weights in zip(pair, pivots(fronts)):
            vx[i] = weights

    def front_update(i):
        g = i // 2
        if i % 2 == 0:
            acc[g, :, :W] = flat(c1[4 + 2 * g:6 + 2 * g]).astype(F32)
            acc[g, :W, W:2 * W] = flat(c2[4 + g]).astype(F32)
            acc[g, :W, 2 * W:] = flat(trx[2 * g, 1]).astype(F32) + flat(trx[2 * g + 1, 1]).astype(F32)
            acc[g, W:, W:] = jnp.zeros((W, 2 * W), F32)
        acc[g] -= dot(flat(c0[i, 1:]), vx[i])

    def pair_weights():
        columns = [acc[g, :, :W].astype(BF) for g in range(2)]
        fronts = [
            (columns[g][:W], acc[g, :W, W:].astype(BF), [inv[4 * g + 1, 0], inv[4 * g + 1, 1]]) for g in range(2)
        ]
        for g, weights in enumerate(pivots(fronts)):
            vg[g] = weights
            acc[g, W:, W:] -= dot(columns[g][W:], weights)

    def last_weights():
        last = [flat(c2[6]).astype(F32), sum(flat(trx[i, 2]).astype(F32) for i in range(NX))]
        last = (jnp.concatenate(last, axis=1) + acc[0, W:, W:] + acc[1, W:, W:]).astype(BF)
        q[6 * W:] = pivots([(last[:, :W], last[:, W:], [inv[3, 0], inv[3, 1]])])[0]

    def pair_factor():
        vh = q[6 * W:]
        for g in range(2):
            q[(4 + g) * W:(5 + g) * W] = (vg[g, :, W:].astype(F32) - dot(vg[g, :, :W], vh)).astype(BF)

    def front_factor(g):
        vh, qb = q[6 * W:], q[(4 + g) * W:(5 + g) * W]
        for i in (2 * g, 2 * g + 1):
            total = vx[i, :, 2 * W:].astype(F32) - dot(vx[i, :, W:2 * W], vh)
            q[i * W:(i + 1) * W] = (total - dot(vx[i, :, :W], qb)).astype(BF)

    pieces.append(wait_top)
    for g in range(2):
        pieces.append(functools.partial(front_weights, g))
        pieces += [functools.partial(front_update, 2 * g + i) for i in range(2)]
    pieces += [pair_weights, last_weights, pair_factor]
    pieces += [functools.partial(front_factor, g) for g in range(2)] + [q_copy.start]

    def finish(b, carry):
        n = 256
        total = sum(flat(xin[i, b]).astype(F32) for i in range(NX))
        for i in range(7):
            block = l0[i, b] if i < 4 else l1[i - 4, b] if i < 6 else l2[b]
            total = total - dot(flat(block), q[i * W:(i + 1) * W])
        kept = (level > 0) | (b * n >= SEP_END)
        out[pl.ds(pl.multiple_of(b * n, n), n), :] = jnp.where(kept, total, 0.0).astype(BF)
        return carry

    def result():
        @pl.when(panel < 3)
        def _():
            inv_load.wait()
            out[...] = jnp.zeros_like(out)

        @pl.when(panel > 2)
        def _():
            @pl.when(c == 1)
            def _():
                inv_load.wait()
                q_copy.wait_recv()

            lax.fori_loop(0, ROWS // 256, finish, 0)

    core_phase()
    flows()
    wait_sums()
    result()
    drain_flows()
    drain_copies()


def solution(mesh):
    def body(contrib, pattern, pivot_inverse):
        anywhere = pl.BlockSpec(memory_space=pl.ANY)
        dma = pltpu.SemaphoreType.DMA
        nf = len(FLOWS)

        def rows(*sizes):
            return pltpu.VMEM((*sizes, 64, W), BF)

        return pl.pallas_call(
            kernel,
            out_shape=jax.ShapeDtypeStruct((ROWS, W), BF),
            in_specs=[anywhere] * 3,
            out_specs=pl.BlockSpec(memory_space=pltpu.VMEM),
            scratch_shapes=[
                pltpu.SMEM((64, 64), jnp.int32),
                pltpu.VMEM((2 * NX * ROWS, W), BF),
                pltpu.VMEM((8, 2, PANEL, PANEL), BF),
                rows(NX, 4, 4), rows(NX, 4, 4), rows(NX, 4, 4), rows(NX, 4, 4), rows(NX, 3, 4),
                rows(3, NX, 4), rows(3, 3), rows(3, NX, 4), rows(3, NX, 3),
                rows(4, 4, 4), rows(2, 4, 4), rows(4, 4), rows(NX, 3, 4), rows(8, 4), rows(8, 4),
                pltpu.VMEM((7 * W, W), BF),
                pltpu.VMEM((NX, W, 3 * W), BF),
                pltpu.VMEM((2, W, 2 * W), BF),
                pltpu.VMEM((2, 2 * W, 3 * W), F32),
                dma((2 * NX + 2,)), dma((NX,)), dma((NX,)), dma((3,)), dma((NX,)), dma((3,)), dma((NX,)),
                dma((4, NX + 1)), dma((3, NX + 1)), dma((3, 2, 3)), dma((3, 2, NX)),
                dma((nf, 4)), dma((nf, KC)), dma((4, 8)), dma((4, 4)), dma((4, 2)),
                dma, dma,
            ],
            compiler_params=pltpu.CompilerParams(
                collective_id=0, has_side_effects=True, vmem_limit_bytes=56 * 1024 * 1024
            ),
        )(pattern[0], contrib[0], pivot_inverse)

    in_specs = (P("level", None, "panel"), P("level", None, None), P())
    return jax.shard_map(body, mesh=mesh, in_specs=in_specs, out_specs=P("level", "panel"), check_vma=False)
```

```python
import functools

import jax
import jax.numpy as jnp
import numpy as np
from jax import lax
from jax.experimental import pallas as pl
from jax.experimental.pallas import tpu as pltpu
from jax.sharding import PartitionSpec as P

MESH = pl.DeviceIdType.MESH
PANEL = 128
W = 256
SEP_END = 3 * W
NX, NC, NY, NZ = 4, 2, 4, 8
ROWS = 1024
BF, F32 = jnp.bfloat16, jnp.float32
TREES = (
    ((0xFE000082, 0x657D0001, 0x07440000, 0xE1240000), (0x55AA55AA, 0xC6113992, 0x38FEFE7C)),
    ((0x0080100C, 0x0A80000E, 0x3810387F, 0x028B0600), (0x55AA55AA, 0xE776E4CC, 0xF8FDFBF0)),
    ((0x007DCF01, 0x0000FE00, 0x40080700, 0x0440E100), (0x55AA55AA, 0xBB93C692, 0xFE7C387C)),
    ((0x00022070, 0x900200F0, 0x80A3C000, 0x181018FD), (0x55AA55AA, 0xCFDC4E66, 0x3E7FBF1E)),
)
DEPTH = 7
FIRST = tuple([mask & 1 for mask in go].index(1) for go, _ in TREES)
FLOWS = tuple((slab, tree) for slab in range(3) for tree in range(4))
KC = 4
LONG = (
    ((5, 6, 7, 9, 10, 11, 12, 13), (9, 10, 11, 12), (9, 11)),
    ((0, 1, 4, 5, 7, 8, 10, 11), (6, 7, 9, 10), (8, 11)),
)
TOPS = ((0, 1, 2, 3), (1, 2, 3, 4), (1, 2, 3, 4))
CROSS = (0, 1, 2, 3)
HOPS = (6, 4)
SLOTS = 22
LAST = max(max(max(slots) for slots in LONG[i]) + (DEPTH - 1) * HOPS[i] // 2 for i in range(NC)) + 1
ELIMINATE = max(max(slots) for slots in TOPS) + 1 + (DEPTH - 1) * HOPS[0] // 2
UNROLL = 1
SPREAD = 3


def dot(a, b):
    return jnp.dot(a, b, preferred_element_type=F32)


def bit_of(word, at):
    return lax.shift_right_logical(word, at) & 1


def bit(mask, at):
    return bit_of(jnp.int32(np.uint32(mask).astype(np.int32)), at)


def at_slot(slots, core, slot):
    taken = bit_of(jnp.where(core == 0, *[jnp.int32(sum(1 << t for t in own)) for own in slots]), slot) == 1
    words = [
        jnp.where(core == 0, *[jnp.int32(sum(k << 3 * (t % 10) for k, t in enumerate(own) if t // 10 == w)) for own in slots])
        for w in range(3)
    ]
    word = jnp.where(slot < 10, words[0], jnp.where(slot < 20, words[1], words[2]))
    return taken, lax.shift_right_logical(word, 3 * lax.rem(slot, 10)) & 7


def pivots(fronts):
    seps, rows, inverses = zip(*fronts)
    n = range(len(fronts))
    first = [dot(inverses[i][0], rows[i][:PANEL]).astype(BF) for i in n]
    between = [dot(inverses[i][0], seps[i][:PANEL, PANEL:]).astype(BF) for i in n]
    second = [(rows[i][PANEL:].astype(F32) - dot(seps[i][PANEL:, :PANEL], first[i])).astype(BF) for i in n]
    second = [dot(inverses[i][1], second[i]).astype(BF) for i in n]
    first = [(first[i].astype(F32) - dot(between[i], second[i])).astype(BF) for i in n]
    return [jnp.concatenate([first[i], second[i]], 0) for i in n]


def kernel(
    pattern_in, contrib, inv_in, out,
    pattern, raw, inv, sent, own, xin, fin, trx, first_l, first_c, cross_l, cross_c,
    l0, l1, l2, c0, c1, c2, q, vx, vg, acc,
    load, core_send, core_recv, trx_send, trx_recv, xin_send, xin_recv,
    root_send, first_recv, cross_send, cross_recv, flow_send, c_recv, l_recv0, l_recv1, l_recv2, q_send, q_recv,
):
    level, panel = lax.axis_index("level"), lax.axis_index("panel")
    x, c = level // NC, level % NC
    y, z = panel // NZ, panel % NZ
    other = (x * NC + 1 - c, panel)
    apart = (2, 1, 3)
    theres = [lax.rem(x + d, NX) for d in apart]
    to_x = [(there * NC + c, panel) for there in theres]
    to = [
        (level, lax.rem(y + 1, NY) * NZ + z),
        (level, lax.rem(y + NY - 1, NY) * NZ + z),
        (level, y * NZ + lax.rem(z + 1, NZ)),
        (level, y * NZ + lax.rem(z + NZ - 1, NZ)),
    ]
    barrier = pltpu.get_barrier_semaphore()
    partners = [other] + to_x + to

    def remote(src, dst, send, recv, device):
        return pltpu.make_async_remote_copy(
            src_ref=src, dst_ref=dst, send_sem=send, recv_sem=recv, device_id=device, device_id_type=MESH
        )

    near = [x] + theres
    top_at = jnp.where(x == 0, 0, jnp.where(x == 2, 1, jnp.where(x == 3, 2, 3)))
    order = [0] + [jnp.where(top_at >= n, near[n - 1], near[n]) for n in range(1, NX)]

    def load_block(i):
        rows = pl.ds(pl.multiple_of((NC * order[i % NX] + jnp.where(i < NX, 1 - c, c)) * ROWS, ROWS), ROWS)
        return pltpu.make_async_copy(contrib.at[rows], raw.at[rows], load.at[i])

    pattern_load = pltpu.make_async_copy(pattern_in, pattern, load.at[2 * NX + 1])
    pattern_load.start()
    loads = [load_block(i) for i in range(2 * NX)]
    for copy in loads:
        copy.start()
    inv_load = pltpu.make_async_copy(inv_in, inv, load.at[2 * NX])
    inv_load.start()
    for partner in partners:
        pl.semaphore_signal(barrier, inc=1, device_id=partner, device_id_type=MESH)

    lane = lax.broadcasted_iota(jnp.int32, (PANEL, W), 1)

    def mask_block(j, parity, store):
        def step(i, carry):
            row = (j * NC + parity) * (ROWS // PANEL) + i
            left = pattern[row, panel * 2].astype(F32)
            right = pattern[row, panel * 2 + 1].astype(F32)
            factor = jnp.where(lane < PANEL, left, right).astype(BF)
            block = raw[pl.ds(pl.multiple_of(row * PANEL, PANEL), PANEL), :] * factor
            store(i // 2, pl.ds(2 * lax.rem(i, 2), 2), block.reshape(2, 64, W))
            return carry

        lax.fori_loop(0, ROWS // PANEL, step, 0, unroll=UNROLL)

    core_copies = [remote(sent.at[j], fin.at[j], core_send.at[n], core_recv.at[n], other) for n, j in enumerate(order)]

    def send_block(n):
        def store(h, half, block):
            sent[order[n], h, half] = block

        loads[n].wait()
        mask_block(order[n], 1 - c, store)
        if n == 0:
            pl.semaphore_wait(barrier, len(partners))
        core_copies[n].start()

    def add_block(n):
        def store(h, half, block):
            own[order[n], h, half] = block + fin[order[n], h, half]

        loads[NX + n].wait()
        core_copies[n].wait_recv()
        mask_block(order[n], c, store)

    places = []
    for slab, tree in FLOWS:
        at = y * NZ + lax.rem(z - slab + NZ, NZ)
        go, deep = TREES[tree]
        depth = bit(deep[0], at) + 2 * bit(deep[1], at) + 4 * bit(deep[2], at)
        places.append((depth, [(bit(mask, at) == 1) & (depth > 0) for mask in go]))
    nexts = []
    for slab in range(3):
        firsts = [places[slab * 4 + tree][0] == 1 for tree in range(4)]
        nexts.append((sum(f.astype(jnp.int32) for f in firsts) > 0, sum(t * f.astype(jnp.int32) for t, f in enumerate(firsts))))
    root = jnp.minimum(panel, 2)

    top_rows = own.at[0, pl.ds(0, 3)]
    trx_copies = [remote(top_rows, trx.at[x], trx_send, trx_recv.at[x], to_x[i]) for i in range(3)]
    xin_copies = [
        remote(own.at[theres[i]], xin.at[x], xin_send, xin_recv.at[x], to_x[i]) for i in range(3)
    ]
    root_c = [
        remote(own.at[0, pl.ds(0, 3), t], first_c.at[root], root_send.at[t], first_recv.at[root, NX], to[FIRST[t]])
        for t in range(4)
    ]
    root_l = [
        [
            remote(own.at[j, :, t], first_l.at[root, j], root_send.at[t], first_recv.at[root, j], to[FIRST[t]])
            for t in range(4)
        ]
        for n, j in enumerate(order)
    ]

    def core_phase():
        pattern_load.wait()
        for n in range(NX):
            send_block(n)
        for n in range(NX):
            add_block(n)

            @pl.when(panel < 3)
            def _():
                if n == 0:
                    @pl.when(c == 0)
                    def _():
                        for copy in root_c:
                            copy.start()

                for copy in root_l[n]:
                    copy.start()

    def cross_copy(slab, i):
        return remote(
            first_l.at[slab, theres[i]], cross_l.at[slab, x],
            cross_send.at[slab], cross_recv.at[slab, 0, x], to_x[i],
        )

    def cross_copy_c(slab, i):
        return remote(
            first_c.at[slab], cross_c.at[slab, x], cross_send.at[slab], cross_recv.at[slab, 1, x], to_x[i]
        )

    def wait_first(slab, j):
        remote(own.at[0, :, 0], first_l.at[slab, j], root_send.at[0], first_recv.at[slab, j], to[0]).wait_recv()

    def wait_cross(slab, there):
        remote(
            first_l.at[slab, 0], cross_l.at[slab, there],
            cross_send.at[slab], cross_recv.at[slab, 0, there], to_x[0],
        ).wait_recv()

    def cross_step(slot):
        for slab in range(3):
            @pl.when(nexts[slab][0] & (c == 0) & (slot == CROSS[0]))
            def _():
                remote(
                    own.at[0, pl.ds(0, 3), 0], first_c.at[slab], root_send.at[0], first_recv.at[slab, NX], to[0]
                ).wait_recv()
                for i in range(3):
                    cross_copy_c(slab, i).start()

            for i in range(3):
                @pl.when(nexts[slab][0] & (slot == CROSS[1 + i]))
                def _():
                    wait_first(slab, theres[i])
                    cross_copy(slab, i).start()

    def x_start():
        @pl.when(c == 0)
        def _():
            for copy in trx_copies:
                copy.start()

        for copy in xin_copies:
            copy.start()

    def wait_sums():
        @pl.when(panel > 2)
        def _():
            xin[x] = own[x]
            for there in theres:
                remote(own.at[0], xin.at[there], xin_send, xin_recv.at[there], to_x[0]).wait_recv()

    def plus(*blocks):
        return sum(block.astype(F32) for block in blocks).astype(BF)

    def wait_cross_c(slab, there):
        remote(
            first_c.at[slab], cross_c.at[slab, there],
            cross_send.at[slab], cross_recv.at[slab, 1, there], to_x[0],
        ).wait_recv()

    def top_blocks(slab):
        tree = nexts[slab][1]
        cross_c[slab, x] = first_c[slab]
        for there in theres:
            wait_cross_c(slab, there)
        ref = (c0, c1, c2)[slab]
        for i in range(NX):
            ref[i, tree] = cross_c[slab, i, 0]
        for g in range(2):
            if slab == 1:
                for h in range(2):
                    c1[4 + 2 * g + h, tree] = plus(cross_c[1, 2 * g, 1 + h], cross_c[1, 2 * g + 1, 1 + h])
            else:
                c2[4 + g, tree] = plus(cross_c[2, 2 * g, 1], cross_c[2, 2 * g + 1, 1])
        if slab == 2:
            c2[6, tree] = plus(*[cross_c[2, i, 2] for i in range(NX)])
            c2[7, tree] = jnp.zeros((64, W), BF)

    def long_sums(slab):
        tree = nexts[slab][1]
        wait_first(slab, x)
        cross_l[slab, x] = first_l[slab, x]
        for there in theres:
            wait_cross(slab, there)
        if slab == 1:
            for g in range(2):
                l1[g, :, tree] = plus(cross_l[1, 2 * g], cross_l[1, 2 * g + 1])
        else:
            l2[:, tree] = plus(*[cross_l[2, i] for i in range(NX)])

    def which(j):
        return lax.rem(x + jnp.where(j == 0, 0, jnp.where(j == 1, 2, jnp.where(j == 2, 3, 1))), NX)

    def prepare(slot):
        cross_step(slot)
        for j in range(NX):
            @pl.when((c == 0) & nexts[0][0] & (slot == TOPS[0][j]))
            def _():
                there = which(j)
                if j == 0:
                    c0[x, :, nexts[0][1]] = first_c[0]
                else:
                    wait_cross_c(0, there)
                    c0[there, :, nexts[0][1]] = cross_c[0, there]

        for slab in (1, 2):
            @pl.when((c == 0) & nexts[slab][0] & (slot == TOPS[slab][0]))
            def _():
                top_blocks(slab)

        for j in range(NX):
            @pl.when(nexts[0][0] & (slot == jnp.where(c == 0, *[LONG[core][0][2 * j] for core in range(NC)])))
            def _():
                there = which(j)
                if j == 0:
                    wait_first(0, x)
                    l0[x, :, nexts[0][1]] = first_l[0, x]
                else:
                    wait_cross(0, there)
                    l0[there, :, nexts[0][1]] = cross_l[0, there]

        for slab in (1, 2):
            @pl.when(nexts[slab][0] & (slot == jnp.where(c == 0, *[LONG[core][slab][0] for core in range(NC)])))
            def _():
                long_sums(slab)

    def top_item(f, k):
        slab, tree = FLOWS[f]
        if slab == 0:
            return c0.at[which(k), :, tree]
        return (c0, c1, c2)[slab].at[pl.ds(2 * k, 2), tree]

    def long_item(f, k):
        slab, tree = FLOWS[f]
        here = pl.ds(2 * lax.rem(k, 2), 2)
        if slab == 0:
            return l0.at[which(k // 2), here, tree]
        if slab == 1:
            return l1.at[k // 2, here, tree]
        return l2.at[here, tree]

    def handle(f, k, item, recv, row):
        depth, go = places[f]
        ref = item(f, k)

        @pl.when(depth > 1)
        def _():
            remote(ref, ref, flow_send.at[f, 0], recv.at[row, k], to[0]).wait_recv()

        for i in range(4):
            @pl.when(go[i])
            def _():
                remote(ref, ref, flow_send.at[f, i], recv.at[row, k], to[i]).start()

    pieces = []
    is_first = nexts[0][0] | nexts[1][0] | nexts[2][0]
    hop = jnp.where(c == 0, *HOPS)

    def step(tau, carry):
        pl.when(is_first & (tau < SLOTS))(functools.partial(prepare, tau))
        pl.when((panel > 2) & (tau == max(CROSS) + 1))(x_start)
        for f, (slab, tree) in enumerate(FLOWS):
            depth = places[f][0]
            slot = tau - (depth - 1) * hop // 2

            @pl.when((depth > 0) & (slot >= 0) & (slot < SLOTS))
            def _():
                is_top, k_top = at_slot((TOPS[slab],) * NC, c, slot)
                is_long, k_long = at_slot((LONG[0][slab], LONG[1][slab]), c, slot)

                @pl.when((c == 0) & is_top)
                def _():
                    handle(f, k_top, top_item, c_recv, f)

                @pl.when(is_long)
                def _():
                    handle(f, k_long, long_item, (l_recv0, l_recv1, l_recv2)[slab], tree)

        @pl.when((c == 0) & (panel > 2) & (tau >= ELIMINATE))
        def _():
            for i, piece in enumerate(pieces):
                when = min(ELIMINATE + i * SPREAD // len(pieces), LAST - 1)
                pl.when(tau == when)(piece)

        return carry

    def flows():
        lax.fori_loop(0, LAST, step, 0)

    def drain_flows():
        for f, (slab, _) in enumerate(FLOWS):
            long_rows = (4, 2, 1)[slab] * ROWS // 4
            top = (SEP_END, 2 * W, 2 * W)[slab]
            for core, rows in ((0, long_rows + top), (1, long_rows)):
                for i in range(4):
                    @pl.when(places[f][1][i] & (c == core))
                    def _():
                        sized = raw.at[pl.ds(0, rows)]
                        remote(sized, sized, flow_send.at[f, i], c_recv.at[f, 0], to[i]).wait_send()

    q_copy = remote(q, q, q_send, q_recv, other)

    def drain_copies():
        def drain(send, rows):
            for core in range(NC):
                @pl.when(c == core)
                def _():
                    sized = raw.at[pl.ds(0, rows[core])]
                    remote(sized, sized, send, q_recv, other).wait_send()

        for copy in core_copies:
            copy.wait_send()

        @pl.when(panel < 3)
        def _():
            for t in range(4):
                drain(root_send.at[t], (ROWS + SEP_END // 4, ROWS))

        for slab in range(3):
            @pl.when(nexts[slab][0])
            def _():
                drain(cross_send.at[slab], (3 * (ROWS + SEP_END) // 4, 3 * ROWS // 4))

        @pl.when(panel > 2)
        def _():
            drain(xin_send, (3 * ROWS, 3 * ROWS))

            @pl.when(c == 0)
            def _():
                q_copy.wait_send()
                sized = raw.at[pl.ds(0, 3 * SEP_END)]
                remote(sized, sized, trx_send, q_recv, other).wait_send()

    def flat(block):
        return block.reshape(-1, W)

    def wait_top():
        inv_load.wait()
        trx[x] = own[0, :3]
        for there in theres:
            remote(top_rows, trx.at[there], trx_send, trx_recv.at[there], to_x[0]).wait_recv()

    def front_weights(g):
        pair = (2 * g, 2 * g + 1)
        fronts = []
        for i in pair:
            rows = jnp.concatenate([flat(c1[i]), flat(c2[i]), flat(trx[i, 0])], axis=1)
            fronts.append((flat(c0[i, 0]), rows, [inv[2 * i, 0], inv[2 * i, 1]]))
        for i, weights in zip(pair, pivots(fronts)):
            vx[i] = weights

    def front_update(i):
        g = i // 2
        if i % 2 == 0:
            acc[g, :, :W] = flat(c1[4 + 2 * g:6 + 2 * g]).astype(F32)
            acc[g, :W, W:2 * W] = flat(c2[4 + g]).astype(F32)
            acc[g, :W, 2 * W:] = flat(trx[2 * g, 1]).astype(F32) + flat(trx[2 * g + 1, 1]).astype(F32)
            acc[g, W:, W:] = jnp.zeros((W, 2 * W), F32)
        acc[g] -= dot(flat(c0[i, 1:]), vx[i])

    def pair_weights():
        columns = [acc[g, :, :W].astype(BF) for g in range(2)]
        fronts = [
            (columns[g][:W], acc[g, :W, W:].astype(BF), [inv[4 * g + 1, 0], inv[4 * g + 1, 1]]) for g in range(2)
        ]
        for g, weights in enumerate(pivots(fronts)):
            vg[g] = weights
            acc[g, W:, W:] -= dot(columns[g][W:], weights)

    def last_weights():
        last = [flat(c2[6]).astype(F32), sum(flat(trx[i, 2]).astype(F32) for i in range(NX))]
        last = (jnp.concatenate(last, axis=1) + acc[0, W:, W:] + acc[1, W:, W:]).astype(BF)
        q[6 * W:] = pivots([(last[:, :W], last[:, W:], [inv[3, 0], inv[3, 1]])])[0]

    def pair_factor():
        vh = q[6 * W:]
        for g in range(2):
            q[(4 + g) * W:(5 + g) * W] = (vg[g, :, W:].astype(F32) - dot(vg[g, :, :W], vh)).astype(BF)

    def front_factor(g):
        vh, qb = q[6 * W:], q[(4 + g) * W:(5 + g) * W]
        for i in (2 * g, 2 * g + 1):
            total = vx[i, :, 2 * W:].astype(F32) - dot(vx[i, :, W:2 * W], vh)
            q[i * W:(i + 1) * W] = (total - dot(vx[i, :, :W], qb)).astype(BF)

    pieces.append(wait_top)
    for g in range(2):
        pieces.append(functools.partial(front_weights, g))
        pieces += [functools.partial(front_update, 2 * g + i) for i in range(2)]
    pieces += [pair_weights, last_weights, pair_factor]
    pieces += [functools.partial(front_factor, g) for g in range(2)] + [q_copy.start]

    def finish(b, carry):
        n = 256
        total = sum(flat(xin[i, b]).astype(F32) for i in range(NX))
        for i in range(7):
            block = l0[i, b] if i < 4 else l1[i - 4, b] if i < 6 else l2[b]
            total = total - dot(flat(block), q[i * W:(i + 1) * W])
        kept = (level > 0) | (b * n >= SEP_END)
        out[pl.ds(pl.multiple_of(b * n, n), n), :] = jnp.where(kept, total, 0.0).astype(BF)
        return carry

    def result():
        @pl.when(panel < 3)
        def _():
            inv_load.wait()
            out[...] = jnp.zeros_like(out)

        @pl.when(panel > 2)
        def _():
            @pl.when(c == 1)
            def _():
                inv_load.wait()
                q_copy.wait_recv()

            lax.fori_loop(0, ROWS // 256, finish, 0)

    core_phase()
    flows()
    wait_sums()
    result()
    drain_flows()
    drain_copies()


def solution(mesh):
    def body(contrib, pattern, pivot_inverse):
        anywhere = pl.BlockSpec(memory_space=pl.ANY)
        dma = pltpu.SemaphoreType.DMA
        nf = len(FLOWS)

        def rows(*sizes):
            return pltpu.VMEM((*sizes, 64, W), BF)

        return pl.pallas_call(
            kernel,
            out_shape=jax.ShapeDtypeStruct((ROWS, W), BF),
            in_specs=[anywhere] * 3,
            out_specs=pl.BlockSpec(memory_space=pltpu.VMEM),
            scratch_shapes=[
                pltpu.SMEM((64, 64), jnp.int32),
                pltpu.VMEM((2 * NX * ROWS, W), BF),
                pltpu.VMEM((8, 2, PANEL, PANEL), BF),
                rows(NX, 4, 4), rows(NX, 4, 4), rows(NX, 4, 4), rows(NX, 4, 4), rows(NX, 3, 4),
                rows(3, NX, 4), rows(3, 3), rows(3, NX, 4), rows(3, NX, 3),
                rows(4, 4, 4), rows(2, 4, 4), rows(4, 4), rows(NX, 3, 4), rows(8, 4), rows(8, 4),
                pltpu.VMEM((7 * W, W), BF),
                pltpu.VMEM((NX, W, 3 * W), BF),
                pltpu.VMEM((2, W, 2 * W), BF),
                pltpu.VMEM((2, 2 * W, 3 * W), F32),
                dma((2 * NX + 2,)), dma((NX,)), dma((NX,)), dma, dma((NX,)), dma, dma((NX,)),
                dma((4,)), dma((3, NX + 1)), dma((3,)), dma((3, 2, NX)),
                dma((nf, 4)), dma((nf, KC)), dma((4, 8)), dma((4, 4)), dma((4, 2)),
                dma, dma,
            ],
            compiler_params=pltpu.CompilerParams(
                collective_id=0, has_side_effects=True, vmem_limit_bytes=56 * 1024 * 1024
            ),
        )(pattern[0], contrib[0], pivot_inverse)

    in_specs = (P("level", None, "panel"), P("level", None, None), P())
    return jax.shard_map(body, mesh=mesh, in_specs=in_specs, out_specs=P("level", "panel"), check_vma=False)
```

```python
import functools

import jax
import jax.numpy as jnp
import numpy as np
from jax import lax
from jax.experimental import pallas as pl
from jax.experimental.pallas import tpu as pltpu
from jax.sharding import PartitionSpec as P

MESH = pl.DeviceIdType.MESH
PANEL = 128
W = 256
SEP_END = 3 * W
NX, NC, NY, NZ = 4, 2, 4, 8
ROWS = 1024
BF, F32 = jnp.bfloat16, jnp.float32
TREES = (
    ((0xFE000082, 0x657D0001, 0x07440000, 0xE1240000), (0x55AA55AA, 0xC6113992, 0x38FEFE7C)),
    ((0x0080100C, 0x0A80000E, 0x3810387F, 0x028B0600), (0x55AA55AA, 0xE776E4CC, 0xF8FDFBF0)),
    ((0x007DCF01, 0x0000FE00, 0x40080700, 0x0440E100), (0x55AA55AA, 0xBB93C692, 0xFE7C387C)),
    ((0x00022070, 0x900200F0, 0x80A3C000, 0x181018FD), (0x55AA55AA, 0xCFDC4E66, 0x3E7FBF1E)),
)
DEPTH = 7
FIRST = tuple([mask & 1 for mask in go].index(1) for go, _ in TREES)
FLOWS = tuple((slab, tree) for slab in range(3) for tree in range(4))
KC = 4
LONG = (
    ((5, 6, 7, 9, 10, 11, 12, 13), (9, 10, 11, 12), (9, 11)),
    ((0, 1, 4, 5, 7, 8, 10, 11), (6, 7, 9, 10), (8, 11)),
)
TOPS = ((0, 1, 2, 3), (1, 2, 3, 4), (1, 2, 3, 4))
CROSS = (0, 1, 2, 3)
HOPS = (6, 4)
SLOTS = 22
LAST = max(max(max(slots) for slots in LONG[i]) + (DEPTH - 1) * HOPS[i] // 2 for i in range(NC)) + 1
ELIMINATE = max(max(slots) for slots in TOPS) + 1 + (DEPTH - 1) * HOPS[0] // 2
UNROLL = 1
SPREAD = 3


def dot(a, b):
    return jnp.dot(a, b, preferred_element_type=F32)


def bit_of(word, at):
    return lax.shift_right_logical(word, at) & 1


def bit(mask, at):
    return bit_of(jnp.int32(np.uint32(mask).astype(np.int32)), at)


def at_slot(slots, core, slot):
    taken = bit_of(jnp.where(core == 0, *[jnp.int32(sum(1 << t for t in own)) for own in slots]), slot) == 1
    words = [
        jnp.where(core == 0, *[jnp.int32(sum(k << 3 * (t % 10) for k, t in enumerate(own) if t // 10 == w)) for own in slots])
        for w in range(3)
    ]
    word = jnp.where(slot < 10, words[0], jnp.where(slot < 20, words[1], words[2]))
    return taken, lax.shift_right_logical(word, 3 * lax.rem(slot, 10)) & 7


def pivots(fronts):
    seps, rows, inverses = zip(*fronts)
    n = range(len(fronts))
    first = [dot(inverses[i][0], rows[i][:PANEL]).astype(BF) for i in n]
    between = [dot(inverses[i][0], seps[i][:PANEL, PANEL:]).astype(BF) for i in n]
    second = [(rows[i][PANEL:].astype(F32) - dot(seps[i][PANEL:, :PANEL], first[i])).astype(BF) for i in n]
    second = [dot(inverses[i][1], second[i]).astype(BF) for i in n]
    first = [(first[i].astype(F32) - dot(between[i], second[i])).astype(BF) for i in n]
    return [jnp.concatenate([first[i], second[i]], 0) for i in n]


def kernel(
    pattern_in, contrib, inv_in, out,
    pattern, raw, inv, sent, own, xin, fin, trx, first_l, first_c, cross_l, cross_c,
    l0, l1, l2, c0, c1, c2, q, vx, vg, acc,
    load, core_send, core_recv, trx_send, trx_recv, xin_send, xin_recv,
    root_send, first_recv, cross_send, cross_recv, flow_send, c_recv, l_recv0, l_recv1, l_recv2, q_send, q_recv,
):
    level, panel = lax.axis_index("level"), lax.axis_index("panel")
    x, c = level // NC, level % NC
    y, z = panel // NZ, panel % NZ
    other = (x * NC + 1 - c, panel)
    apart = (2, 1, 3)
    theres = [lax.rem(x + d, NX) for d in apart]
    to_x = [(there * NC + c, panel) for there in theres]
    to = [
        (level, lax.rem(y + 1, NY) * NZ + z),
        (level, lax.rem(y + NY - 1, NY) * NZ + z),
        (level, y * NZ + lax.rem(z + 1, NZ)),
        (level, y * NZ + lax.rem(z + NZ - 1, NZ)),
    ]
    barrier = pltpu.get_barrier_semaphore()
    partners = [other] + to_x + to

    def remote(src, dst, send, recv, device):
        return pltpu.make_async_remote_copy(
            src_ref=src, dst_ref=dst, send_sem=send, recv_sem=recv, device_id=device, device_id_type=MESH
        )

    near = [x] + theres
    top_at = jnp.where(x == 0, 0, jnp.where(x == 2, 1, jnp.where(x == 3, 2, 3)))
    order = [0] + [jnp.where(top_at >= n, near[n - 1], near[n]) for n in range(1, NX)]

    def load_block(i):
        rows = pl.ds(pl.multiple_of((NC * order[i % NX] + jnp.where(i < NX, 1 - c, c)) * ROWS, ROWS), ROWS)
        return pltpu.make_async_copy(contrib.at[rows], raw.at[rows], load.at[i])

    pattern_load = pltpu.make_async_copy(pattern_in, pattern, load.at[2 * NX + 1])
    pattern_load.start()
    loads = [load_block(i) for i in range(2 * NX)]
    for copy in loads:
        copy.start()
    inv_load = pltpu.make_async_copy(inv_in, inv, load.at[2 * NX])
    inv_load.start()
    for partner in partners:
        pl.semaphore_signal(barrier, inc=1, device_id=partner, device_id_type=MESH)

    lane = lax.broadcasted_iota(jnp.int32, (PANEL, W), 1)

    def mask_block(j, parity, store):
        def step(i, carry):
            row = (j * NC + parity) * (ROWS // PANEL) + i
            left = pattern[row, panel * 2].astype(F32)
            right = pattern[row, panel * 2 + 1].astype(F32)
            factor = jnp.where(lane < PANEL, left, right).astype(BF)
            block = raw[pl.ds(pl.multiple_of(row * PANEL, PANEL), PANEL), :] * factor
            store(i // 2, pl.ds(2 * lax.rem(i, 2), 2), block.reshape(2, 64, W))
            return carry

        lax.fori_loop(0, ROWS // PANEL, step, 0, unroll=UNROLL)

    core_copies = [remote(sent.at[j], fin.at[j], core_send, core_recv.at[n], other) for n, j in enumerate(order)]

    def send_block(n):
        def store(h, half, block):
            sent[order[n], h, half] = block

        loads[n].wait()
        mask_block(order[n], 1 - c, store)
        if n == 0:
            pl.semaphore_wait(barrier, len(partners))
        core_copies[n].start()

    def add_block(n):
        def store(h, half, block):
            own[order[n], h, half] = block + fin[order[n], h, half]

        loads[NX + n].wait()
        core_copies[n].wait_recv()
        mask_block(order[n], c, store)

    places = []
    for slab, tree in FLOWS:
        at = y * NZ + lax.rem(z - slab + NZ, NZ)
        go, deep = TREES[tree]
        depth = bit(deep[0], at) + 2 * bit(deep[1], at) + 4 * bit(deep[2], at)
        places.append((depth, [(bit(mask, at) == 1) & (depth > 0) for mask in go]))
    nexts = []
    for slab in range(3):
        firsts = [places[slab * 4 + tree][0] == 1 for tree in range(4)]
        nexts.append((sum(f.astype(jnp.int32) for f in firsts) > 0, sum(t * f.astype(jnp.int32) for t, f in enumerate(firsts))))
    root = jnp.minimum(panel, 2)

    top_rows = own.at[0, pl.ds(0, 3)]
    trx_copies = [remote(top_rows, trx.at[x], trx_send, trx_recv.at[x], to_x[i]) for i in range(3)]
    xin_copies = [
        remote(own.at[theres[i]], xin.at[x], xin_send, xin_recv.at[x], to_x[i]) for i in range(3)
    ]
    root_c = [
        remote(own.at[0, pl.ds(0, 3), t], first_c.at[root], root_send.at[t], first_recv.at[root, NX], to[FIRST[t]])
        for t in range(4)
    ]
    root_l = [
        [
            remote(own.at[j, :, t], first_l.at[root, j], root_send.at[t], first_recv.at[root, j], to[FIRST[t]])
            for t in range(4)
        ]
        for n, j in enumerate(order)
    ]

    def core_phase():
        pattern_load.wait()
        for n in range(NX):
            send_block(n)
        for n in range(NX):
            add_block(n)

            @pl.when(panel < 3)
            def _():
                if n == 0:
                    @pl.when(c == 0)
                    def _():
                        for copy in root_c:
                            copy.start()

                for copy in root_l[n]:
                    copy.start()

    def cross_copy(slab, i):
        return remote(
            first_l.at[slab, theres[i]], cross_l.at[slab, x],
            cross_send.at[slab], cross_recv.at[slab, 0, x], to_x[i],
        )

    def cross_copy_c(slab, i):
        return remote(
            first_c.at[slab], cross_c.at[slab, x], cross_send.at[slab], cross_recv.at[slab, 1, x], to_x[i]
        )

    def wait_first(slab, j):
        remote(own.at[0, :, 0], first_l.at[slab, j], root_send.at[0], first_recv.at[slab, j], to[0]).wait_recv()

    def wait_cross(slab, there):
        remote(
            first_l.at[slab, 0], cross_l.at[slab, there],
            cross_send.at[slab], cross_recv.at[slab, 0, there], to_x[0],
        ).wait_recv()

    def cross_step(slot):
        for slab in range(3):
            @pl.when(nexts[slab][0] & (c == 0) & (slot == CROSS[0]))
            def _():
                remote(
                    own.at[0, pl.ds(0, 3), 0], first_c.at[slab], root_send.at[0], first_recv.at[slab, NX], to[0]
                ).wait_recv()
                for i in range(3):
                    cross_copy_c(slab, i).start()

            for i in range(3):
                @pl.when(nexts[slab][0] & (slot == CROSS[1 + i]))
                def _():
                    wait_first(slab, theres[i])
                    cross_copy(slab, i).start()

    def x_start():
        @pl.when(c == 0)
        def _():
            for copy in trx_copies:
                copy.start()

        for copy in xin_copies:
            copy.start()

    def wait_sums():
        @pl.when(panel > 2)
        def _():
            xin[x] = own[x]
            for there in theres:
                remote(own.at[0], xin.at[there], xin_send, xin_recv.at[there], to_x[0]).wait_recv()

    def plus(*blocks):
        return sum(block.astype(F32) for block in blocks).astype(BF)

    def wait_cross_c(slab, there):
        remote(
            first_c.at[slab], cross_c.at[slab, there],
            cross_send.at[slab], cross_recv.at[slab, 1, there], to_x[0],
        ).wait_recv()

    def top_blocks(slab):
        tree = nexts[slab][1]
        cross_c[slab, x] = first_c[slab]
        for there in theres:
            wait_cross_c(slab, there)
        ref = (c0, c1, c2)[slab]
        for i in range(NX):
            ref[i, tree] = cross_c[slab, i, 0]
        for g in range(2):
            if slab == 1:
                for h in range(2):
                    c1[4 + 2 * g + h, tree] = plus(cross_c[1, 2 * g, 1 + h], cross_c[1, 2 * g + 1, 1 + h])
            else:
                c2[4 + g, tree] = plus(cross_c[2, 2 * g, 1], cross_c[2, 2 * g + 1, 1])
        if slab == 2:
            c2[6, tree] = plus(*[cross_c[2, i, 2] for i in range(NX)])
            c2[7, tree] = jnp.zeros((64, W), BF)

    def long_sums(slab):
        tree = nexts[slab][1]
        wait_first(slab, x)
        if slab == 1:
            cross_l[slab, x] = first_l[slab, x]
        for there in theres:
            wait_cross(slab, there)
        if slab == 1:
            for g in range(2):
                l1[g, :, tree] = plus(cross_l[1, 2 * g], cross_l[1, 2 * g + 1])
        else:
            l2[:, tree] = plus(first_l[2, x], *[cross_l[2, there] for there in theres])

    def which(j):
        return lax.rem(x + jnp.where(j == 0, 0, jnp.where(j == 1, 2, jnp.where(j == 2, 3, 1))), NX)

    def prepare(slot):
        cross_step(slot)
        for j in range(NX):
            @pl.when((c == 0) & nexts[0][0] & (slot == TOPS[0][j]))
            def _():
                there = which(j)
                if j == 0:
                    c0[x, :, nexts[0][1]] = first_c[0]
                else:
                    wait_cross_c(0, there)
                    c0[there, :, nexts[0][1]] = cross_c[0, there]

        for slab in (1, 2):
            @pl.when((c == 0) & nexts[slab][0] & (slot == TOPS[slab][0]))
            def _():
                top_blocks(slab)

        for j in range(NX):
            @pl.when(nexts[0][0] & (slot == jnp.where(c == 0, *[LONG[core][0][2 * j] for core in range(NC)])))
            def _():
                there = which(j)
                if j == 0:
                    wait_first(0, x)
                    l0[x, :, nexts[0][1]] = first_l[0, x]
                else:
                    wait_cross(0, there)
                    l0[there, :, nexts[0][1]] = cross_l[0, there]

        for slab in (1, 2):
            @pl.when(nexts[slab][0] & (slot == jnp.where(c == 0, *[LONG[core][slab][0] for core in range(NC)])))
            def _():
                long_sums(slab)

    def top_item(f, k):
        slab, tree = FLOWS[f]
        if slab == 0:
            return c0.at[which(k), :, tree]
        return (c0, c1, c2)[slab].at[pl.ds(2 * k, 2), tree]

    def long_item(f, k):
        slab, tree = FLOWS[f]
        here = pl.ds(2 * lax.rem(k, 2), 2)
        if slab == 0:
            return l0.at[which(k // 2), here, tree]
        if slab == 1:
            return l1.at[k // 2, here, tree]
        return l2.at[here, tree]

    def handle(f, k, item, recv, row):
        depth, go = places[f]
        ref = item(f, k)

        @pl.when(depth > 1)
        def _():
            remote(ref, ref, flow_send.at[f, 0], recv.at[row, k], to[0]).wait_recv()

        for i in range(4):
            @pl.when(go[i])
            def _():
                remote(ref, ref, flow_send.at[f, i], recv.at[row, k], to[i]).start()

    pieces = []
    is_first = nexts[0][0] | nexts[1][0] | nexts[2][0]
    hop = jnp.where(c == 0, *HOPS)

    def step(tau, carry):
        pl.when(is_first & (tau < SLOTS))(functools.partial(prepare, tau))
        pl.when((panel > 2) & (tau == max(CROSS) + 1))(x_start)
        for f, (slab, tree) in enumerate(FLOWS):
            depth = places[f][0]
            slot = tau - (depth - 1) * hop // 2

            @pl.when((depth > 0) & (slot >= 0) & (slot < SLOTS))
            def _():
                is_top, k_top = at_slot((TOPS[slab],) * NC, c, slot)
                is_long, k_long = at_slot((LONG[0][slab], LONG[1][slab]), c, slot)

                @pl.when((c == 0) & is_top)
                def _():
                    handle(f, k_top, top_item, c_recv, f)

                @pl.when(is_long)
                def _():
                    handle(f, k_long, long_item, (l_recv0, l_recv1, l_recv2)[slab], tree)

        @pl.when((c == 0) & (panel > 2) & (tau >= ELIMINATE))
        def _():
            for i, piece in enumerate(pieces):
                when = min(ELIMINATE + i * SPREAD // len(pieces), LAST - 1)
                pl.when(tau == when)(piece)

        return carry

    def flows():
        lax.fori_loop(0, LAST, step, 0)

    def drain_flows():
        for f, (slab, _) in enumerate(FLOWS):
            long_rows = (4, 2, 1)[slab] * ROWS // 4
            top = (SEP_END, 2 * W, 2 * W)[slab]
            for core, rows in ((0, long_rows + top), (1, long_rows)):
                for i in range(4):
                    @pl.when(places[f][1][i] & (c == core))
                    def _():
                        sized = raw.at[pl.ds(0, rows)]
                        remote(sized, sized, flow_send.at[f, i], c_recv.at[f, 0], to[i]).wait_send()

    q_copy = remote(q, q, q_send, q_recv, other)

    def drain_copies():
        def drain(send, rows):
            for core in range(NC):
                @pl.when(c == core)
                def _():
                    sized = raw.at[pl.ds(0, rows[core])]
                    remote(sized, sized, send, q_recv, other).wait_send()

        drain(core_send, (NX * ROWS, NX * ROWS))

        @pl.when(panel < 3)
        def _():
            for t in range(4):
                drain(root_send.at[t], (ROWS + SEP_END // 4, ROWS))

        for slab in range(3):
            @pl.when(nexts[slab][0])
            def _():
                drain(cross_send.at[slab], (3 * (ROWS + SEP_END) // 4, 3 * ROWS // 4))

        @pl.when(panel > 2)
        def _():
            drain(xin_send, (3 * ROWS, 3 * ROWS))

            @pl.when(c == 0)
            def _():
                q_copy.wait_send()
                sized = raw.at[pl.ds(0, 3 * SEP_END)]
                remote(sized, sized, trx_send, q_recv, other).wait_send()

    def flat(block):
        return block.reshape(-1, W)

    def wait_top():
        inv_load.wait()
        trx[x] = own[0, :3]
        for there in theres:
            remote(top_rows, trx.at[there], trx_send, trx_recv.at[there], to_x[0]).wait_recv()

    def front_weights(g):
        pair = (2 * g, 2 * g + 1)
        fronts = []
        for i in pair:
            rows = jnp.concatenate([flat(c1[i]), flat(c2[i]), flat(trx[i, 0])], axis=1)
            fronts.append((flat(c0[i, 0]), rows, [inv[2 * i, 0], inv[2 * i, 1]]))
        for i, weights in zip(pair, pivots(fronts)):
            vx[i] = weights

    def front_update(i):
        g = i // 2
        if i % 2 == 0:
            acc[g, :, :W] = flat(c1[4 + 2 * g:6 + 2 * g]).astype(F32)
            acc[g, :W, W:2 * W] = flat(c2[4 + g]).astype(F32)
            acc[g, :W, 2 * W:] = flat(trx[2 * g, 1]).astype(F32) + flat(trx[2 * g + 1, 1]).astype(F32)
            acc[g, W:, W:] = jnp.zeros((W, 2 * W), F32)
        acc[g] -= dot(flat(c0[i, 1:]), vx[i])

    def pair_weights():
        columns = [acc[g, :, :W].astype(BF) for g in range(2)]
        fronts = [
            (columns[g][:W], acc[g, :W, W:].astype(BF), [inv[4 * g + 1, 0], inv[4 * g + 1, 1]]) for g in range(2)
        ]
        for g, weights in enumerate(pivots(fronts)):
            vg[g] = weights
            acc[g, W:, W:] -= dot(columns[g][W:], weights)

    def last_weights():
        last = [flat(c2[6]).astype(F32), sum(flat(trx[i, 2]).astype(F32) for i in range(NX))]
        last = (jnp.concatenate(last, axis=1) + acc[0, W:, W:] + acc[1, W:, W:]).astype(BF)
        q[6 * W:] = pivots([(last[:, :W], last[:, W:], [inv[3, 0], inv[3, 1]])])[0]

    def pair_factor():
        vh = q[6 * W:]
        for g in range(2):
            q[(4 + g) * W:(5 + g) * W] = (vg[g, :, W:].astype(F32) - dot(vg[g, :, :W], vh)).astype(BF)

    def front_factor(g):
        vh, qb = q[6 * W:], q[(4 + g) * W:(5 + g) * W]
        for i in (2 * g, 2 * g + 1):
            total = vx[i, :, 2 * W:].astype(F32) - dot(vx[i, :, W:2 * W], vh)
            q[i * W:(i + 1) * W] = (total - dot(vx[i, :, :W], qb)).astype(BF)

    pieces.append(wait_top)
    for g in range(2):
        pieces.append(functools.partial(front_weights, g))
        pieces += [functools.partial(front_update, 2 * g + i) for i in range(2)]
    pieces += [pair_weights, last_weights, pair_factor]
    pieces += [functools.partial(front_factor, g) for g in range(2)] + [q_copy.start]

    def finish(b, carry):
        n = 256
        total = sum(flat(xin[i, b]).astype(F32) for i in range(NX))
        for i in range(7):
            block = l0[i, b] if i < 4 else l1[i - 4, b] if i < 6 else l2[b]
            total = total - dot(flat(block), q[i * W:(i + 1) * W])
        kept = (level > 0) | (b * n >= SEP_END)
        out[pl.ds(pl.multiple_of(b * n, n), n), :] = jnp.where(kept, total, 0.0).astype(BF)
        return carry

    def result():
        @pl.when(panel < 3)
        def _():
            inv_load.wait()
            out[...] = jnp.zeros_like(out)

        @pl.when(panel > 2)
        def _():
            @pl.when(c == 1)
            def _():
                inv_load.wait()
                q_copy.wait_recv()

            lax.fori_loop(0, ROWS // 256, finish, 0)

    core_phase()
    flows()
    wait_sums()
    result()
    drain_flows()
    drain_copies()


def solution(mesh):
    def body(contrib, pattern, pivot_inverse):
        anywhere = pl.BlockSpec(memory_space=pl.ANY)
        dma = pltpu.SemaphoreType.DMA
        nf = len(FLOWS)

        def rows(*sizes):
            return pltpu.VMEM((*sizes, 64, W), BF)

        return pl.pallas_call(
            kernel,
            out_shape=jax.ShapeDtypeStruct((ROWS, W), BF),
            in_specs=[anywhere] * 3,
            out_specs=pl.BlockSpec(memory_space=pltpu.VMEM),
            scratch_shapes=[
                pltpu.SMEM((64, 64), jnp.int32),
                pltpu.VMEM((2 * NX * ROWS, W), BF),
                pltpu.VMEM((8, 2, PANEL, PANEL), BF),
                rows(NX, 4, 4), rows(NX, 4, 4), rows(NX, 4, 4), rows(NX, 4, 4), rows(NX, 3, 4),
                rows(3, NX, 4), rows(3, 3), rows(3, NX, 4), rows(3, NX, 3),
                rows(4, 4, 4), rows(2, 4, 4), rows(4, 4), rows(NX, 3, 4), rows(8, 4), rows(8, 4),
                pltpu.VMEM((7 * W, W), BF),
                pltpu.VMEM((NX, W, 3 * W), BF),
                pltpu.VMEM((2, W, 2 * W), BF),
                pltpu.VMEM((2, 2 * W, 3 * W), F32),
                dma((2 * NX + 2,)), dma, dma((NX,)), dma, dma((NX,)), dma, dma((NX,)),
                dma((4,)), dma((3, NX + 1)), dma((3,)), dma((3, 2, NX)),
                dma((nf, 4)), dma((nf, KC)), dma((4, 8)), dma((4, 4)), dma((4, 2)),
                dma, dma,
            ],
            compiler_params=pltpu.CompilerParams(
                collective_id=0, has_side_effects=True, vmem_limit_bytes=56 * 1024 * 1024
            ),
        )(pattern[0], contrib[0], pivot_inverse)

    in_specs = (P("level", None, "panel"), P("level", None, None), P())
    return jax.shard_map(body, mesh=mesh, in_specs=in_specs, out_specs=P("level", "panel"), check_vma=False)
```
